32 devices in a mesh: groups: 2 (over x), ctx: 4 (over y, core), heads: 4 (over z).
Axes of the slice: x: 2, y: 2, z: 4, core: 2. Of those that a mesh axis runs over, the one named last changes fastest.
Arguments:
- tokens: bfloat16 [4096, 2048], P(('groups', 'ctx', 'heads')), parts along dimension 0, may hold values from -60 to 60
- state_in: float32 [4, 256, 128], P('heads', 'groups'), parts along dimension 1, may hold values from -256 to 256
- past_kv: bfloat16 [2, 1024, 512], P(None, 'groups', 'heads'), parts along dimension 1, may hold values from -6 to 6
- w_qkv: bfloat16 [2048, 3, 512], P(None, None, 'heads'), may hold values from -0.125 to 0.125
- w_out: bfloat16 [512, 2048], P('heads'), may hold values from -0.25 to 0.25
- w_gate: bfloat16 [16, 2048, 768], P(('ctx', 'heads')), may hold values from -0.125 to 0.125
- w_up: bfloat16 [16, 2048, 768], P(('ctx', 'heads')), may hold values from -0.125 to 0.125
- w_down: bfloat16 [16, 768, 2048], P(('ctx', 'heads')), may hold values from -0.21875 to 0.21875
- expert_ids: int32 [4096, 8], P(('groups', 'ctx', 'heads')), parts along dimension 0, may hold values from 0 to 15, all different within a row; in each aligned block of 128 rows (0 to 127, 128 to 255, ...) at most 128 rows name the same one
- gate_weights: float32 [4096, 8], P(('groups', 'ctx', 'heads')), parts along dimension 0, may hold values from 0.1 to 1
Outputs:
- mixed: bfloat16 [4096, 2048], P(('groups', 'ctx', 'heads')), parts along dimension 0
The draws below stay inside these ranges and needn't reach their ends.
There are 2 independent parts, one for each index of `groups`. The reference program is written for one: setup_inputs(seed, part) draws one part's arguments, and reference() takes and returns one part's arrays. A program takes and returns all parts, laid end to end along the dimension named above; an argument that names none is the same for every part. Nothing has to cross between parts.
Inputs may be any that keep to these rules, and one draw needn't show every extreme that they name: `expert_ids`: each row names 8 different experts; in each aligned block of 128 rows (the rows of one device) no expert is named by more than 128 rows, a bound that some block reaches.
All inputs are finite; a program needn't handle non-finite values.
Results may differ from the reference program's by a relative error of at most 0.017.
Values may be sent and summed in bfloat16 or wider, within the bound.
No kernel may reach another device: no remote copies, remote signals or barrier semaphores. Data moves between devices by JAX's collectives and lax.ppermute only.
A program may use at most 128 MiB of HBM per device.

```python
import math
import jax
import jax.numpy as jnp
import numpy as np
from jax import lax

D = 2048
HDIM = 128
INNER = 768
TOP = 8
WINDOW = 512
TOK_DEV = 512
TOKENS = 2048
ROWS = 128
HEADS = 4
EXPERTS = 16
CAP = 128


def draw_tokens(key, part):
    base_key = jax.random.fold_in(jax.random.fold_in(key, 11), 0)
    values = jax.random.normal(base_key, (TOKENS, D), jnp.float32)
    return jnp.clip(values, -60.0, 60.0).astype(jnp.bfloat16)


def block_scale(stream_key, dims, shards, low, largest):
    def one(axis_at, parts):
        draws = jax.random.uniform(jax.random.fold_in(jax.random.fold_in(stream_key, 6), axis_at), (parts,), jnp.float32, low / len(shards), largest / len(shards))
        return jnp.repeat(jnp.exp(draws), dims[axis_at] // parts).reshape((-1,) + (1,) * (len(dims) - axis_at - 1))

    gain = one(*shards[0])
    for cut in shards[1:]:
        gain = gain * one(*cut)
    return gain


def routed_block(key, own, number, rows, amount, top, most, slope):
    sequence = jax.random.permutation(key, amount)
    crowded, common = shares(amount, rows * top, most, slope, True), shares(amount, rows * top, most, slope, False)
    places = jnp.arange(amount)

    def named(tallies, offset_by):
        used = int((tallies > 0).sum())
        fixed = max(1, used // 4)
        shifted = fixed + (places - fixed + offset_by * (used - fixed)) % max(1, amount - fixed)
        return jnp.zeros((amount,), jnp.int32).at[sequence[jnp.where(places < fixed, places, shifted)]].set(jnp.asarray(tallies, jnp.int32))

    tallies = jnp.where(number % 4 == 0, named(crowded, number // 4), named(common, number - number // 4 - 1))
    mixed = jax.random.permutation(jax.random.fold_in(own, 3), amount)
    source_of, taker = mixed[0:amount // 2 * 2:2], mixed[1:amount // 2 * 2:2]
    room = jnp.minimum(tallies[source_of] - 1, most - tallies[taker]) // 2
    room = jnp.where((source_of == sequence[0]) | (taker == sequence[0]) | (tallies[taker] == 0), 0, jnp.maximum(room, 0))
    shifted = jax.random.randint(jax.random.fold_in(own, 4), (amount // 2,), 0, 1 << 20) % (room + 1)
    tallies = tallies.at[source_of].add(-shifted).at[taker].add(shifted)
    labels = jnp.searchsorted(jnp.cumsum(tallies), jnp.arange(rows * top), side="right").astype(jnp.int32)
    grid = labels.reshape(top, rows).T
    grid = grid[jax.random.permutation(jax.random.fold_in(own, 1), rows)]
    offset_by = jax.random.randint(jax.random.fold_in(own, 2), (rows, 1), 0, top)
    return jnp.take_along_axis(grid, (jnp.arange(top)[None, :] + offset_by) % top, axis=1)


def shares(number_of, total, limit, slope, full):
    portions = [(1 << 20) // math.isqrt(grade ** slope) + 1 for grade in range(1, number_of + 1)]
    largest = limit if full else min(limit, max(-(-total // number_of), total * portions[0] // sum(portions)))
    least = 1 if total - largest >= number_of - 1 else 0
    given, rest = [largest] + [least] * (number_of - 1), total - largest - least * (number_of - 1)
    while rest > 0:
        candidates = [i for i in range(1, number_of) if given[i] < largest] or [i for i in range(1, number_of) if given[i] < limit]
        whole, left = sum([portions[i] for i in candidates]), rest
        for i in candidates:
            more = min(limit - given[i], max(1, left * portions[i] // whole), rest)
            given[i] = given[i] + more
            rest = rest - more
    return np.array(given)


def normal_values(stream_key, dims, scale, bound, cuts=(), kind=jnp.bfloat16):
    result = scale * jax.random.normal(stream_key, dims, jnp.float32)
    if cuts:
        result = result * block_scale(stream_key, dims, cuts, -0.22, 0.18)
    return jnp.clip(result, -bound, bound).astype(kind)


def setup_inputs(seed: int = 0, part: int = 0) -> dict:
    splits = jax.random.split(jax.random.key(seed), 11)
    own_keys = jax.random.split(jax.random.fold_in(splits[10], part), 11)
    tokens = draw_tokens(jax.random.fold_in(jax.random.fold_in(splits[10], part), 71), part)
    state_in = normal_values(own_keys[1], (HEADS, HDIM, HDIM), (TOKENS ** 0.5), 256.0, ((0, 4),), jnp.float32)
    past_kv = normal_values(own_keys[2], (2, WINDOW, HEADS * HDIM), 1.0, 6.0, ((2, 4),))
    w_qkv = normal_values(splits[3], (D, 3, HEADS * HDIM), D ** -0.5, 0.125, ((2, 4),))
    w_out = normal_values(splits[4], (HEADS * HDIM, D), (HEADS * HDIM) ** -0.5, 0.25, ((0, 4),))
    w_gate = normal_values(splits[5], (EXPERTS, D, INNER), D ** -0.5, 0.125, ((0, 16),))
    w_up = normal_values(splits[6], (EXPERTS, D, INNER), D ** -0.5, 0.125, ((0, 16),))
    w_down = normal_values(splits[7], (EXPERTS, INNER, D), INNER ** -0.5, 0.21875, ((0, 16),))
    expert_ids_keys = jax.random.split(jax.random.fold_in(own_keys[8], 1), TOKENS // ROWS)
    expert_ids_turns = jax.random.permutation(jax.random.fold_in(own_keys[8], 3), TOKENS // ROWS)
    expert_ids = jax.vmap(lambda own, number: routed_block(jax.random.fold_in(own_keys[8], 2), own, number, ROWS, EXPERTS, TOP, CAP, 2))(expert_ids_keys, expert_ids_turns).reshape((TOKENS, TOP))
    gate_weights = jnp.clip(jnp.exp(math.log(1.0) - 2.3025851 * jax.random.uniform(own_keys[9], (TOKENS, TOP), jnp.float32) ** block_scale(own_keys[9], (TOKENS, TOP), ((0, 16),), -0.2, 0.2)), 0.1, 1.0)
    return dict(tokens=tokens, state_in=state_in, past_kv=past_kv, w_qkv=w_qkv, w_out=w_out, w_gate=w_gate, w_up=w_up, w_down=w_down, expert_ids=expert_ids, gate_weights=gate_weights)


def normalize(value):
    return value * lax.rsqrt(lax.optimization_barrier(jnp.mean(value * value, axis=-1, keepdims=True)) + 1e-06)

def one_head(query, keys, values, start_state, past_keys, past_values):
    block_rows = min(TOK_DEV, 512)
    block_count = TOKENS // block_rows
    scale = 1.0 / math.sqrt(HDIM)
    causal = jnp.arange(block_rows)[:, None] >= jnp.arange(block_rows)[None, :]
    offsets = jnp.arange(WINDOW + block_rows)[None, :] - jnp.arange(block_rows)[:, None]
    in_window = (offsets > 0) & (offsets <= WINDOW)
    all_keys = jnp.concatenate([past_keys, keys], axis=0)
    all_values = jnp.concatenate([past_values, values], axis=0)

    def step(state, index):
        first = (index * block_rows).astype(jnp.int32)
        q_block = lax.dynamic_slice_in_dim(query, first, block_rows, 0)
        k_block = lax.dynamic_slice_in_dim(keys, first, block_rows, 0)
        v_block = lax.dynamic_slice_in_dim(values, first, block_rows, 0)
        carried = jnp.dot(q_block.astype(jnp.float32), state, precision=lax.Precision.HIGHEST)
        inside = jnp.dot(q_block, k_block.T, preferred_element_type=jnp.float32)
        inside = jnp.where(causal, inside, 0.0).astype(jnp.bfloat16)
        linear = carried + jnp.dot(inside, v_block, preferred_element_type=jnp.float32)
        w_keys = lax.dynamic_slice_in_dim(all_keys, first, WINDOW + block_rows, 0)
        w_values = lax.dynamic_slice_in_dim(all_values, first, WINDOW + block_rows, 0)
        scores = jnp.dot(q_block, w_keys.T, preferred_element_type=jnp.float32) * scale
        scores = jnp.where(in_window, scores, -jnp.inf)
        top_score = lax.optimization_barrier(jnp.max(scores, axis=-1, keepdims=True))
        expo = jnp.exp(scores - top_score)
        probs = (expo / lax.optimization_barrier(jnp.sum(expo, axis=-1, keepdims=True))).astype(jnp.bfloat16)
        window_out = jnp.dot(probs, w_values, preferred_element_type=jnp.float32)
        combined = (normalize(linear) + window_out).astype(jnp.bfloat16)
        new_state = state + jnp.dot(k_block.T, v_block, preferred_element_type=jnp.float32)
        return (new_state, combined)
    _, outs = lax.scan(step, start_state, jnp.arange(block_count, dtype=jnp.int32))
    return outs.reshape(TOKENS, HDIM)

def slot_block(block_ids):
    onehot = (block_ids[:, None] == jnp.arange(EXPERTS, dtype=jnp.int32)[None, :]).astype(jnp.int32)
    earlier = jnp.cumsum(onehot, axis=0) - onehot
    return lax.optimization_barrier(jnp.sum(onehot * earlier, axis=1)).astype(jnp.int32)

def reference(tokens, state_in, past_kv, w_qkv, w_out, w_gate, w_up, w_down, expert_ids, gate_weights):
    projected = jnp.dot(tokens, w_qkv.reshape(D, 3 * HEADS * HDIM), preferred_element_type=jnp.float32)
    projected = projected.astype(jnp.bfloat16).reshape(TOKENS, 3, HEADS, HDIM)
    query = jnp.transpose(projected[:, 0], (1, 0, 2))
    keys = jnp.transpose(projected[:, 1], (1, 0, 2))
    values = jnp.transpose(projected[:, 2], (1, 0, 2))
    past = jnp.transpose(past_kv.reshape(2, WINDOW, HEADS, HDIM), (0, 2, 1, 3))

    def per_head(inputs):
        return one_head(*inputs)
    heads_out = lax.map(per_head, (query, keys, values, state_in, past[0], past[1]))
    heads_out = jnp.transpose(heads_out, (1, 0, 2)).reshape(TOKENS, HEADS * HDIM)
    attn = jnp.dot(heads_out, w_out, preferred_element_type=jnp.float32)
    hidden_state = (tokens.astype(jnp.float32) + attn).astype(jnp.bfloat16)
    normed = normalize(hidden_state.astype(jnp.float32)).astype(jnp.bfloat16)
    sources = TOKENS // ROWS
    picks = expert_ids.reshape(sources, ROWS * TOP).astype(jnp.int32)
    slots = lax.map(slot_block, picks)
    source_ids = jnp.broadcast_to(jnp.arange(sources, dtype=jnp.int32)[:, None], picks.shape)
    token_ids = source_ids * ROWS + (jnp.arange(ROWS * TOP, dtype=jnp.int32) // TOP)[None, :]
    table = jnp.full((EXPERTS, sources, CAP), TOKENS, jnp.int32).at[picks, source_ids, slots].set(token_ids)
    weight_table = jnp.zeros((EXPERTS, sources, CAP), jnp.float32).at[picks, source_ids, slots].set(gate_weights.reshape(sources, ROWS * TOP))
    padded = jnp.concatenate([normed, jnp.zeros((1, D), jnp.bfloat16)], axis=0)

    def expert_step(total, inputs):
        index_rows, weight_rows, gate_mat, up_mat, down_mat = inputs
        flat_index = index_rows.reshape(-1)
        rows_in = padded[flat_index]
        gate_act = jnp.dot(rows_in, gate_mat, preferred_element_type=jnp.float32)
        up_act = jnp.dot(rows_in, up_mat, preferred_element_type=jnp.float32)
        hid = (jax.nn.silu(gate_act) * up_act).astype(jnp.bfloat16)
        out_rows = jnp.dot(hid, down_mat, preferred_element_type=jnp.float32).astype(jnp.bfloat16)
        total = total.at[flat_index].add(weight_rows.reshape(-1)[:, None] * out_rows.astype(jnp.float32))
        return (total, None)
    total, _ = lax.scan(expert_step, jnp.zeros((TOKENS + 1, D), jnp.float32), (table, weight_table, w_gate, w_up, w_down))
    return (hidden_state.astype(jnp.float32) + total[:TOKENS]).astype(jnp.bfloat16)
```

```python
import math

import jax
import jax.numpy as jnp
from jax import lax
from jax.sharding import PartitionSpec as P

HDIM = 128
WINDOW = 512


def entering(x, axis, join, neutral):
    place = lax.axis_index(axis)
    gathered = lax.all_gather(x.astype(jnp.bfloat16), axis)
    state = jnp.zeros_like(x) + jnp.asarray(neutral, x.dtype)

    def one(lap, state):
        return join(state, lax.dynamic_index_in_dim(gathered, lap, 0, False).astype(x.dtype))

    return lax.fori_loop(0, place, one, state)


def from_behind(block, axis, distance):
    devices = range(lax.axis_size(axis))
    route = [(i - distance, i) for i in devices if i - distance in devices]
    return lax.ppermute(block, axis, route)


def normalize(value):
    return value * lax.rsqrt(jnp.mean(value * value, axis=-1, keepdims=True) + 1e-06)


def on_device_routed(
    tokens, state_in, past_kv, w_qkv, w_out, w_gate, w_up, w_down, expert_ids, gate_weights
):
    row_count, model_width = tokens.shape
    inner_width = w_qkv.shape[2]
    local_heads = inner_width // HDIM
    w_flat = w_qkv.reshape(model_width, 3 * inner_width)
    projected = jnp.dot(
        lax.all_gather(tokens, "heads", axis=0, tiled=True),
        w_flat,
        preferred_element_type=jnp.float32,
    ).astype(jnp.bfloat16)
    slab_rows = projected.shape[0]
    projected = projected.reshape(slab_rows, 3, local_heads, HDIM)
    query = jnp.transpose(projected[:, 0], (1, 0, 2))
    keys = jnp.transpose(projected[:, 1], (1, 0, 2))
    values = jnp.transpose(projected[:, 2], (1, 0, 2))
    local_state = jnp.einsum("hsd,hse->hde", keys, values, preferred_element_type=jnp.float32)
    earlier_state = entering(
        local_state, "ctx", lambda first, second: first + second, jnp.zeros_like(local_state)
    )
    start_state = state_in + earlier_state
    tail = jnp.stack([keys, values], axis=0)
    arrived = from_behind(tail, "ctx", 1)
    past = jnp.transpose(past_kv.reshape(2, WINDOW, local_heads, HDIM), (0, 2, 1, 3))
    previous = jnp.where(lax.axis_index("ctx") == 0, past, arrived)
    all_keys = jnp.concatenate([previous[0], keys], axis=1)
    all_values = jnp.concatenate([previous[1], values], axis=1)
    block_rows = min(slab_rows, 512)
    block_count = slab_rows // block_rows
    scale = 1.0 / math.sqrt(HDIM)
    causal = jnp.arange(block_rows)[:, None] >= jnp.arange(block_rows)[None, :]
    offsets = jnp.arange(WINDOW + block_rows)[None, :] - jnp.arange(block_rows)[:, None]
    in_window = (offsets > 0) & (offsets <= WINDOW)

    def block_step(state, index):
        first = index * block_rows
        carried = jnp.einsum(
            "hsd,hde->hse", query.astype(jnp.float32), state, precision=lax.Precision.HIGHEST
        )
        inside = jnp.einsum("hsd,htd->hst", query, keys, preferred_element_type=jnp.float32)
        inside = jnp.where(causal[None], inside, 0.0).astype(jnp.bfloat16)
        linear = carried + jnp.einsum(
            "hst,hte->hse", inside, values, preferred_element_type=jnp.float32
        )
        scores = (
            jnp.einsum("hsd,htd->hst", query, all_keys, preferred_element_type=jnp.float32) * scale
        )
        scores = jnp.where(in_window[None], scores, -jnp.inf)
        top_score = jnp.max(scores, axis=-1, keepdims=True)
        expo = jnp.exp(scores - top_score)
        probs = (expo / jnp.sum(expo, axis=-1, keepdims=True)).astype(jnp.bfloat16)
        window_out = jnp.einsum(
            "hst,hte->hse", probs, all_values, preferred_element_type=jnp.float32
        )
        combined = (normalize(linear) + window_out).astype(jnp.bfloat16)
        new_state = state + jnp.einsum(
            "hsd,hse->hde", keys, values, preferred_element_type=jnp.float32
        )
        return (new_state, combined)

    _, outs = lax.scan(block_step, start_state, jnp.arange(block_count, dtype=jnp.int32))
    heads_out = jnp.transpose(outs, (0, 2, 1, 3)).reshape(slab_rows, inner_width)
    regrouped = lax.all_to_all(heads_out, "heads", split_axis=0, concat_axis=1, tiled=True)
    attn = jnp.dot(
        regrouped,
        lax.all_gather(w_out, "heads", axis=0, tiled=True),
        preferred_element_type=jnp.float32,
    )
    hidden_state = (tokens.astype(jnp.float32) + attn).astype(jnp.bfloat16)
    hidden_float = hidden_state.astype(jnp.float32)
    normed = normalize(hidden_float).astype(jnp.bfloat16)
    ctx_count = lax.axis_size("ctx")
    head_count = lax.axis_size("heads")
    exp_local = w_gate.shape[0]
    expert_count = exp_local * ctx_count * head_count
    top_count = expert_ids.shape[1]
    capacity = max(2, 2 * row_count * top_count // expert_count)
    picks = expert_ids.reshape(-1)
    onehot = (picks[:, None] == jnp.arange(expert_count, dtype=jnp.int32)[None, :]).astype(
        jnp.int32
    )
    earlier = jnp.cumsum(onehot, axis=0) - onehot
    slots = jnp.sum(onehot * earlier, axis=1)
    destination = picks * capacity + slots
    source_rows = jnp.arange(row_count * top_count, dtype=jnp.int32) // top_count
    outgoing = jnp.zeros((expert_count * capacity, model_width), jnp.bfloat16)
    outgoing = outgoing.at[destination].set(normed[source_rows])
    sendable = outgoing.reshape(expert_count, 1, capacity, model_width)
    arrived_rows = lax.all_to_all(
        sendable, ("ctx", "heads"), split_axis=0, concat_axis=1, tiled=True
    )
    e_count, n_count, c_count, d_count = arrived_rows.shape
    flat = arrived_rows.reshape(e_count, n_count * c_count, d_count)
    gate_act = jnp.einsum("erd,edf->erf", flat, w_gate, preferred_element_type=jnp.float32)
    up_act = jnp.einsum("erd,edf->erf", flat, w_up, preferred_element_type=jnp.float32)
    hid = (jax.nn.silu(gate_act) * up_act).astype(jnp.bfloat16)
    out_rows = jnp.einsum("erf,efd->erd", hid, w_down, preferred_element_type=jnp.float32)
    finished = out_rows.astype(jnp.bfloat16).reshape(e_count, n_count, c_count, d_count)
    returned = lax.all_to_all(finished, ("ctx", "heads"), split_axis=1, concat_axis=0, tiled=True)
    returned = returned.reshape(expert_count * capacity, model_width)
    picked = returned[destination].reshape(row_count, top_count, model_width).astype(jnp.float32)
    routed = jnp.sum(gate_weights[:, :, None] * picked, axis=1)
    return (hidden_float + routed).astype(jnp.bfloat16)


def ring_pairs(count, step):
    return [(i, (i + step) % count) for i in range(count)]


def partner_pairs(count, bit):
    return [(i, i ^ bit) for i in range(count)]


def gather_ring(block, count):
    blocks = [block]
    for _ in range(count - 1):
        blocks.append(lax.ppermute(blocks[-1], "heads", ring_pairs(count, 1)))
    return blocks


def gather_direct(block, count):
    return [block] + [
        lax.ppermute(block, "heads", ring_pairs(count, step)) for step in range(1, count)
    ]


def flip_row(block, ctx_count):
    return lax.ppermute(block, "ctx", partner_pairs(ctx_count, 2))


def flip_core(block, ctx_count):
    return lax.ppermute(block, "ctx", partner_pairs(ctx_count, 1))


def gather_w_out(w_out, head_count, ctx_count, group_count):
    rows = w_out.shape[0]
    parts = 2 * group_count
    piece_rows = rows // parts
    core = lax.axis_index("ctx") % 2
    place = core * group_count + lax.axis_index("groups")
    piece = lax.dynamic_slice_in_dim(w_out, place * piece_rows, piece_rows, 0)
    own = jnp.stack(gather_direct(piece, head_count), axis=0)[:, None]
    if group_count == 2:
        other = lax.ppermute(own, "groups", [(0, 1), (1, 0)])
        first = lax.axis_index("groups") == 0
        own = jnp.concatenate(
            [jnp.where(first, own, other), jnp.where(first, other, own)], axis=1
        )
    other = flip_core(own, ctx_count)
    own = jnp.concatenate(
        [jnp.where(core == 0, own, other), jnp.where(core == 0, other, own)], axis=1
    )
    return own.reshape(head_count * rows, w_out.shape[1])


def on_device_dense(
    tokens, state_in, past_kv, w_qkv, w_out, w_gate, w_up, w_down, expert_ids, gate_weights
):
    row_count, model_width = tokens.shape
    head_count = lax.axis_size("heads")
    ctx_count = lax.axis_size("ctx")
    group_count = lax.axis_size("groups")
    ctx = lax.axis_index("ctx")
    place = lax.axis_index("heads")
    slab_rows = row_count * head_count
    expert_count = ctx_count * head_count
    starts = [((place - s) % head_count) * row_count for s in range(head_count)]

    hit = expert_ids[:, :, None] == jnp.arange(expert_count, dtype=jnp.int32)[None, None, :]
    dense_weights = jnp.sum(jnp.where(hit, gate_weights[:, :, None], 0.0), axis=1)
    all_weights = lax.all_gather(dense_weights, ("ctx", "heads"), axis=0, tiled=True)
    all_weights = all_weights.reshape(ctx_count, slab_rows, expert_count)

    blocks = gather_ring(tokens, head_count)
    w_flat = w_qkv.reshape(model_width, 3 * HDIM)
    projected = jnp.zeros((slab_rows, 3 * HDIM), jnp.bfloat16)
    for s in range(head_count):
        part = jnp.dot(blocks[s], w_flat, preferred_element_type=jnp.float32)
        projected = lax.dynamic_update_slice_in_dim(
            projected, part.astype(jnp.bfloat16), starts[s], 0
        )
    across = [flip_row(block, ctx_count) for block in blocks]
    w_out_all = gather_w_out(w_out, head_count, ctx_count, group_count)
    experts = [
        (w_gate[0], w_up[0], w_down[0]),
        tuple(flip_core(w[0], ctx_count) for w in (w_gate, w_up, w_down)),
    ]

    query = projected[:, :HDIM]
    keys = projected[:, HDIM : 2 * HDIM]
    values = projected[:, 2 * HDIM :]
    local_state = jnp.dot(keys.T, values, preferred_element_type=jnp.float32)
    arrived = from_behind(projected[:, HDIM:], "ctx", 1)
    start_state = state_in[0]
    packed_state = local_state.astype(jnp.bfloat16)
    for distance in range(1, ctx_count):
        start_state = start_state + from_behind(packed_state, "ctx", distance).astype(jnp.float32)
    past = jnp.concatenate([past_kv[0], past_kv[1]], axis=1)
    previous = jnp.where(ctx == 0, past, arrived)
    all_keys = jnp.concatenate([previous[:, :HDIM], keys], axis=0)
    all_values = jnp.concatenate([previous[:, HDIM:], values], axis=0)
    scale = 1.0 / math.sqrt(HDIM)
    causal = jnp.arange(slab_rows)[:, None] >= jnp.arange(slab_rows)[None, :]
    offsets = jnp.arange(WINDOW + slab_rows)[None, :] - jnp.arange(slab_rows)[:, None]
    in_window = (offsets > 0) & (offsets <= WINDOW)
    carried = jnp.dot(
        query.astype(jnp.float32), start_state, precision=lax.Precision.HIGHEST
    )
    products = jnp.dot(query, all_keys.T, preferred_element_type=jnp.float32)
    inside = jnp.where(causal, products[:, WINDOW:], 0.0).astype(jnp.bfloat16)
    linear = carried + jnp.dot(inside, values, preferred_element_type=jnp.float32)
    scores = jnp.where(in_window, products * scale, -jnp.inf)
    expo = jnp.exp(scores - jnp.max(scores, axis=-1, keepdims=True))
    probs = (expo / jnp.sum(expo, axis=-1, keepdims=True)).astype(jnp.bfloat16)
    window_out = jnp.dot(probs, all_values, preferred_element_type=jnp.float32)
    heads_out = (normalize(linear) + window_out).astype(jnp.bfloat16)

    near_heads = gather_direct(heads_out, head_count)
    far_heads = [flip_row(part, ctx_count) for part in near_heads]

    own_expert = ctx * head_count + place
    other_expert = (ctx ^ 1) * head_count + place

    def chunk_rows(s):
        heads_rows = jnp.concatenate(
            [
                jnp.concatenate(
                    [lax.dynamic_slice_in_dim(part, starts[s], row_count, 0) for part in parts],
                    axis=1,
                )
                for parts in (near_heads, far_heads)
            ],
            axis=0,
        )
        token_rows = jnp.concatenate([blocks[s], across[s]], axis=0)
        attn = jnp.dot(heads_rows, w_out_all, preferred_element_type=jnp.float32)
        hidden = (token_rows.astype(jnp.float32) + attn).astype(jnp.bfloat16)
        return hidden, normalize(hidden.astype(jnp.float32)).astype(jnp.bfloat16)

    def chunk_weights(s, expert):
        rows = [
            lax.dynamic_slice(all_weights, (where, starts[s], expert), (1, row_count, 1))
            for where in (ctx, ctx ^ 2)
        ]
        return jnp.concatenate(rows, axis=1)[0]

    def chunk_sum(s, normed):
        total = 0.0
        for (gate, up, down), expert in zip(experts, (own_expert, other_expert)):
            gate_act = jnp.dot(normed, gate, preferred_element_type=jnp.float32)
            up_act = jnp.dot(normed, up, preferred_element_type=jnp.float32)
            hid = (jax.nn.silu(gate_act) * up_act).astype(jnp.bfloat16)
            out_rows = jnp.dot(hid, down, preferred_element_type=jnp.float32)
            out_rows = out_rows.astype(jnp.bfloat16).astype(jnp.float32)
            total = total + chunk_weights(s, expert) * out_rows
        return total.astype(jnp.bfloat16)

    carry = None
    for s in list(range(1, head_count)) + [0]:
        hidden, normed = chunk_rows(s)
        partial = chunk_sum(s, normed)
        near, far = partial[:row_count], partial[row_count:]
        joined = near.astype(jnp.float32) + flip_row(far, ctx_count).astype(jnp.float32)
        if carry is not None:
            joined = joined + carry.astype(jnp.float32)
        if s:
            carry = lax.ppermute(
                joined.astype(jnp.bfloat16), "heads", ring_pairs(head_count, 1)
            )
    return (hidden[:row_count].astype(jnp.float32) + joined).astype(jnp.bfloat16)


def solution(mesh):
    sizes = mesh.shape

    def on_device(*args):
        w_qkv, w_gate, expert_ids = args[3], args[5], args[8]
        expert_count = w_gate.shape[0] * sizes["ctx"] * sizes["heads"]
        slab_rows = args[0].shape[0] * sizes["heads"]
        dense = (
            sizes["ctx"] == 4
            and sizes["groups"] <= 2
            and w_gate.shape[0] == 1
            and w_qkv.shape[2] == HDIM
            and slab_rows == WINDOW
            and expert_count <= 2 * expert_ids.shape[1]
        )
        return (on_device_dense if dense else on_device_routed)(*args)

    return jax.shard_map(
        on_device,
        mesh=mesh,
        in_specs=(
            P(("groups", "ctx", "heads"), None),
            P("heads", "groups", None),
            P(None, "groups", "heads"),
            P(None, None, "heads"),
            P("heads", None),
            P(("ctx", "heads"), None, None),
            P(("ctx", "heads"), None, None),
            P(("ctx", "heads"), None, None),
            P(("groups", "ctx", "heads"), None),
            P(("groups", "ctx", "heads"), None),
        ),
        out_specs=P(("groups", "ctx", "heads"), None),
        check_vma=False,
    )
```

```python
import functools
import math

import jax
import jax.numpy as jnp
from jax import lax
from jax.experimental import pallas as pl
from jax.experimental.pallas import tpu as pltpu
from jax.sharding import PartitionSpec as P

HDIM = 128
WINDOW = 512


def entering(x, axis, join, neutral):
    place = lax.axis_index(axis)
    gathered = lax.all_gather(x.astype(jnp.bfloat16), axis)
    state = jnp.zeros_like(x) + jnp.asarray(neutral, x.dtype)

    def one(lap, state):
        return join(state, lax.dynamic_index_in_dim(gathered, lap, 0, False).astype(x.dtype))

    return lax.fori_loop(0, place, one, state)


def from_behind(block, axis, distance):
    devices = range(lax.axis_size(axis))
    route = [(i - distance, i) for i in devices if i - distance in devices]
    return lax.ppermute(block, axis, route)


def normalize(value):
    return value * lax.rsqrt(jnp.mean(value * value, axis=-1, keepdims=True) + 1e-06)


def on_device_routed(
    tokens, state_in, past_kv, w_qkv, w_out, w_gate, w_up, w_down, expert_ids, gate_weights
):
    row_count, model_width = tokens.shape
    inner_width = w_qkv.shape[2]
    local_heads = inner_width // HDIM
    w_flat = w_qkv.reshape(model_width, 3 * inner_width)
    projected = jnp.dot(
        lax.all_gather(tokens, "heads", axis=0, tiled=True),
        w_flat,
        preferred_element_type=jnp.float32,
    ).astype(jnp.bfloat16)
    slab_rows = projected.shape[0]
    projected = projected.reshape(slab_rows, 3, local_heads, HDIM)
    query = jnp.transpose(projected[:, 0], (1, 0, 2))
    keys = jnp.transpose(projected[:, 1], (1, 0, 2))
    values = jnp.transpose(projected[:, 2], (1, 0, 2))
    local_state = jnp.einsum("hsd,hse->hde", keys, values, preferred_element_type=jnp.float32)
    earlier_state = entering(
        local_state, "ctx", lambda first, second: first + second, jnp.zeros_like(local_state)
    )
    start_state = state_in + earlier_state
    tail = jnp.stack([keys, values], axis=0)
    arrived = from_behind(tail, "ctx", 1)
    past = jnp.transpose(past_kv.reshape(2, WINDOW, local_heads, HDIM), (0, 2, 1, 3))
    previous = jnp.where(lax.axis_index("ctx") == 0, past, arrived)
    all_keys = jnp.concatenate([previous[0], keys], axis=1)
    all_values = jnp.concatenate([previous[1], values], axis=1)
    block_rows = min(slab_rows, 512)
    block_count = slab_rows // block_rows
    scale = 1.0 / math.sqrt(HDIM)
    causal = jnp.arange(block_rows)[:, None] >= jnp.arange(block_rows)[None, :]
    offsets = jnp.arange(WINDOW + block_rows)[None, :] - jnp.arange(block_rows)[:, None]
    in_window = (offsets > 0) & (offsets <= WINDOW)

    def block_step(state, index):
        first = index * block_rows
        carried = jnp.einsum(
            "hsd,hde->hse", query.astype(jnp.float32), state, precision=lax.Precision.HIGHEST
        )
        inside = jnp.einsum("hsd,htd->hst", query, keys, preferred_element_type=jnp.float32)
        inside = jnp.where(causal[None], inside, 0.0).astype(jnp.bfloat16)
        linear = carried + jnp.einsum(
            "hst,hte->hse", inside, values, preferred_element_type=jnp.float32
        )
        scores = (
            jnp.einsum("hsd,htd->hst", query, all_keys, preferred_element_type=jnp.float32) * scale
        )
        scores = jnp.where(in_window[None], scores, -jnp.inf)
        top_score = jnp.max(scores, axis=-1, keepdims=True)
        expo = jnp.exp(scores - top_score)
        probs = (expo / jnp.sum(expo, axis=-1, keepdims=True)).astype(jnp.bfloat16)
        window_out = jnp.einsum(
            "hst,hte->hse", probs, all_values, preferred_element_type=jnp.float32
        )
        combined = (normalize(linear) + window_out).astype(jnp.bfloat16)
        new_state = state + jnp.einsum(
            "hsd,hse->hde", keys, values, preferred_element_type=jnp.float32
        )
        return (new_state, combined)

    _, outs = lax.scan(block_step, start_state, jnp.arange(block_count, dtype=jnp.int32))
    heads_out = jnp.transpose(outs, (0, 2, 1, 3)).reshape(slab_rows, inner_width)
    regrouped = lax.all_to_all(heads_out, "heads", split_axis=0, concat_axis=1, tiled=True)
    attn = jnp.dot(
        regrouped,
        lax.all_gather(w_out, "heads", axis=0, tiled=True),
        preferred_element_type=jnp.float32,
    )
    hidden_state = (tokens.astype(jnp.float32) + attn).astype(jnp.bfloat16)
    hidden_float = hidden_state.astype(jnp.float32)
    normed = normalize(hidden_float).astype(jnp.bfloat16)
    ctx_count = lax.axis_size("ctx")
    head_count = lax.axis_size("heads")
    exp_local = w_gate.shape[0]
    expert_count = exp_local * ctx_count * head_count
    top_count = expert_ids.shape[1]
    capacity = max(2, 2 * row_count * top_count // expert_count)
    picks = expert_ids.reshape(-1)
    onehot = (picks[:, None] == jnp.arange(expert_count, dtype=jnp.int32)[None, :]).astype(
        jnp.int32
    )
    earlier = jnp.cumsum(onehot, axis=0) - onehot
    slots = jnp.sum(onehot * earlier, axis=1)
    destination = picks * capacity + slots
    source_rows = jnp.arange(row_count * top_count, dtype=jnp.int32) // top_count
    outgoing = jnp.zeros((expert_count * capacity, model_width), jnp.bfloat16)
    outgoing = outgoing.at[destination].set(normed[source_rows])
    sendable = outgoing.reshape(expert_count, 1, capacity, model_width)
    arrived_rows = lax.all_to_all(
        sendable, ("ctx", "heads"), split_axis=0, concat_axis=1, tiled=True
    )
    e_count, n_count, c_count, d_count = arrived_rows.shape
    flat = arrived_rows.reshape(e_count, n_count * c_count, d_count)
    gate_act = jnp.einsum("erd,edf->erf", flat, w_gate, preferred_element_type=jnp.float32)
    up_act = jnp.einsum("erd,edf->erf", flat, w_up, preferred_element_type=jnp.float32)
    hid = (jax.nn.silu(gate_act) * up_act).astype(jnp.bfloat16)
    out_rows = jnp.einsum("erf,efd->erd", hid, w_down, preferred_element_type=jnp.float32)
    finished = out_rows.astype(jnp.bfloat16).reshape(e_count, n_count, c_count, d_count)
    returned = lax.all_to_all(finished, ("ctx", "heads"), split_axis=1, concat_axis=0, tiled=True)
    returned = returned.reshape(expert_count * capacity, model_width)
    picked = returned[destination].reshape(row_count, top_count, model_width).astype(jnp.float32)
    routed = jnp.sum(gate_weights[:, :, None] * picked, axis=1)
    return (hidden_float + routed).astype(jnp.bfloat16)


def ring_pairs(count, step):
    return [(i, (i + step) % count) for i in range(count)]


def partner_pairs(count, bit):
    return [(i, i ^ bit) for i in range(count)]


def after(value, *others):
    return lax.optimization_barrier((value, *others))[0]


def next_place(block, count):
    return lax.ppermute(block, "heads", ring_pairs(count, 1))


def gather_direct(block, count):
    return [block] + [
        lax.ppermute(block, "heads", ring_pairs(count, step)) for step in range(1, count)
    ]


def flip_row(block, ctx_count):
    return lax.ppermute(block, "ctx", partner_pairs(ctx_count, 2))


def flip_core(block, ctx_count):
    return lax.ppermute(block, "ctx", partner_pairs(ctx_count, 1))


def w_out_piece(w_out, group_count):
    piece_rows = w_out.shape[0] // (2 * group_count)
    place = (lax.axis_index("ctx") % 2) * group_count + lax.axis_index("groups")
    return lax.dynamic_slice_in_dim(w_out, place * piece_rows, piece_rows, 0)


def chunk_kernel(head_count, turn, place_ref, *refs):
    near_heads = refs[:head_count]
    far_heads = refs[head_count : 2 * head_count]
    near_tokens, far_tokens, near_out_w, far_out_w, *weights = refs[
        2 * head_count : 2 * head_count + 10
    ]
    outs = refs[2 * head_count + 10 : -10]
    heads_buf, token_buf, mark_buf, w_out_buf, *rest = refs[-10:]
    wide_bufs, narrow_bufs, normed_buf, total_buf, small_sems, weight_sems = rest
    row_count, model_width = outs[0].shape
    slab_rows = row_count * head_count
    experts, mark_rows = narrow_bufs.shape[0], mark_buf.shape[1]
    first = pl.multiple_of(place_ref[0], row_count)

    pairs = []
    for side, (heads_in, tokens_in) in enumerate(
        ((near_heads, near_tokens), (far_heads, far_tokens))
    ):
        rows = pl.ds(side * row_count, row_count)
        for turns in range(head_count):
            source = heads_in[turns].at[pl.ds(first, row_count)]
            pairs.append((source, heads_buf.at[rows, pl.ds(turns * HDIM, HDIM)]))
        pairs.append((tokens_in, token_buf.at[rows]))
        pairs.append((heads_in[turn].at[pl.ds(slab_rows, mark_rows)], mark_buf.at[side]))
    group_count = near_out_w.shape[0]
    for core, pieces in enumerate((near_out_w, far_out_w)):
        for group in range(group_count):
            slot = place_ref[3 + core * group_count + group]
            pairs.append((pieces.at[group], w_out_buf.at[:, slot]))
    small = [
        pltpu.make_async_copy(source, target, small_sems.at[i])
        for i, (source, target) in enumerate(pairs)
    ]
    large = []
    for expert in range(experts):
        targets = (wide_bufs.at[expert, 0], wide_bufs.at[expert, 1], narrow_bufs.at[expert])
        for kind, target in enumerate(targets):
            copy = pltpu.make_async_copy(
                weights[3 * expert + kind].at[0], target, weight_sems.at[3 * expert + kind]
            )
            large.append(copy)

    for copy in small:
        copy.start()
    large[0].start()
    for copy in small:
        copy.wait()
    large[1].start()

    w_out_rows = w_out_buf[...].reshape(head_count * HDIM, model_width)
    attn = jnp.dot(heads_buf[...], w_out_rows, preferred_element_type=jnp.float32)
    hidden = (token_buf[...].astype(jnp.float32) + attn).astype(jnp.bfloat16)
    if len(outs) == 3:
        outs[2][...] = hidden[:row_count]
    normed_buf[...] = normalize(hidden.astype(jnp.float32)).astype(jnp.bfloat16)

    spots = lax.rem(lax.broadcasted_iota(jnp.int32, (mark_rows, HDIM), 0), mark_rows // 2)
    for expert in range(experts):
        chosen = jnp.where(spots == place_ref[1 + expert], 1.0, 0.0).astype(jnp.bfloat16)
        gating = jnp.concatenate(
            [
                lax.dot_general(
                    mark_buf[side],
                    chosen,
                    (((0,), (0,)), ((), ())),
                    preferred_element_type=jnp.float32,
                )[:, :1]
                for side in range(2)
            ],
            axis=0,
        )
        acts = []
        for kind in range(3):
            step = 3 * expert + kind
            if step + 2 < len(large):
                large[step + 2].start()
            large[step].wait()
            if kind < 2:
                acts.append(
                    jnp.dot(
                        normed_buf[...], wide_bufs[expert, kind], preferred_element_type=jnp.float32
                    )
                )
        hid = (jax.nn.silu(acts[0]) * acts[1]).astype(jnp.bfloat16)
        rows = jnp.dot(hid, narrow_bufs[expert], preferred_element_type=jnp.float32)
        rows = rows.astype(jnp.bfloat16).astype(jnp.float32) * gating
        if expert:
            rows = rows + total_buf[...]
        if expert < experts - 1:
            total_buf[...] = rows
        else:
            rows = rows.astype(jnp.bfloat16)
            outs[0][...] = rows[:row_count]
            outs[1][...] = rows[row_count:]


def run_chunk(turn, place, near_heads, far_heads, near_tokens, far_tokens, w_out, weights):
    row_count, model_width = near_tokens.shape
    head_count = len(near_heads)
    inner = weights[0].shape[2]
    rows = 2 * row_count
    mark_rows = near_heads[0].shape[0] - row_count * head_count
    experts = len(weights) // 3
    outs = 2 if turn else 3
    anywhere = pl.BlockSpec(memory_space=pl.ANY)
    operands = [*near_heads, *far_heads, near_tokens, far_tokens, *w_out, *weights]
    group_count, _, piece_rows, _ = w_out[0].shape
    flops = 2 * rows * model_width * (3 * experts * inner + head_count * HDIM)
    return pl.pallas_call(
        functools.partial(chunk_kernel, head_count, turn),
        out_shape=[jax.ShapeDtypeStruct((row_count, model_width), jnp.bfloat16)] * outs,
        in_specs=[pl.BlockSpec(memory_space=pltpu.SMEM)] + [anywhere] * len(operands),
        out_specs=[pl.BlockSpec(memory_space=pltpu.VMEM)] * outs,
        scratch_shapes=[
            pltpu.VMEM((rows, head_count * HDIM), jnp.bfloat16),
            pltpu.VMEM((rows, model_width), jnp.bfloat16),
            pltpu.VMEM((2, mark_rows, row_count), jnp.bfloat16),
            pltpu.VMEM((head_count, 2 * group_count, piece_rows, model_width), jnp.bfloat16),
            pltpu.VMEM((experts, 2, model_width, inner), jnp.bfloat16),
            pltpu.VMEM((experts, inner, model_width), jnp.bfloat16),
            pltpu.VMEM((rows, model_width), jnp.bfloat16),
            pltpu.VMEM((rows, model_width), jnp.float32),
            pltpu.SemaphoreType.DMA((2 * (head_count + 2 + group_count),)),
            pltpu.SemaphoreType.DMA((3 * experts,)),
        ],
        compiler_params=pltpu.CompilerParams(vmem_limit_bytes=60 * 2**20),
        cost_estimate=pl.CostEstimate(
            flops=flops, bytes_accessed=sum(2 * math.prod(w.shape) for w in weights), transcendentals=0
        ),
        name="chunk",
    )(place, *operands)


def on_device_dense(
    tokens, state_in, past_kv, w_qkv, w_out, w_gate, w_up, w_down, expert_ids, gate_weights
):
    row_count, model_width = tokens.shape
    head_count = lax.axis_size("heads")
    ctx_count = lax.axis_size("ctx")
    group_count = lax.axis_size("groups")
    ctx = lax.axis_index("ctx")
    place = lax.axis_index("heads")
    slab_rows = row_count * head_count
    expert_count = ctx_count * head_count
    starts = [((place - s) % head_count) * row_count for s in range(head_count)]

    hit = expert_ids[:, :, None] == jnp.arange(expert_count, dtype=jnp.int32)[None, None, :]
    dense_weights = jnp.sum(jnp.where(hit, gate_weights[:, :, None], 0.0), axis=1)
    coarse = lax.reduce_precision(dense_weights, 8, 7)
    halves = [coarse, dense_weights - coarse]
    marks = jnp.concatenate(halves, axis=1).astype(jnp.bfloat16).T

    w_flat = w_qkv.reshape(model_width, 3 * HDIM)
    projected = jnp.zeros((slab_rows, 3 * HDIM), jnp.bfloat16)

    def project(projected, s):
        part = jnp.dot(blocks[s], w_flat, preferred_element_type=jnp.float32)
        return lax.dynamic_update_slice_in_dim(projected, part.astype(jnp.bfloat16), starts[s], 0)

    experts = [w_gate, w_up, w_down]
    blocks, across, swapped = [tokens], [], []
    pieces = [w_out_piece(w_out, group_count)] + [None] * (head_count - 1)
    for s in range(head_count - 1):
        blocks.append(next_place(blocks[s], head_count))
        across.append(flip_row(blocks[s], ctx_count))
        swapped.append(flip_core(after(experts[s], blocks[s]), ctx_count))
        projected = project(projected, s)
        for distance in ((1, head_count - 1), range(2, head_count - 1), ())[s]:
            piece = after(pieces[0], blocks[s], swapped[s])
            pieces[distance] = lax.ppermute(piece, "heads", ring_pairs(head_count, distance))
        extra = (pieces, halves)[s - 1] if s else []
        blocks[-1], across[-1], swapped[-1], projected, *extra = lax.optimization_barrier(
            (blocks[-1], across[-1], swapped[-1], projected, *extra)
        )
        if s == 1:
            halves = [jnp.concatenate(extra, axis=0)]
            if group_count == 2:
                halves.append(lax.ppermute(halves[0], "groups", [(0, 1), (1, 0)]))
    half = jnp.stack(extra, axis=0)
    projected = project(projected, head_count - 1)
    experts = experts + swapped

    query = projected[:, :HDIM]
    keys = projected[:, HDIM : 2 * HDIM]
    values = projected[:, 2 * HDIM :]
    local_state = jnp.dot(keys.T, values, preferred_element_type=jnp.float32)
    arrived = from_behind(projected[:, HDIM:], "ctx", 1)
    start_state = state_in[0]
    packed_state = local_state.astype(jnp.bfloat16)
    for distance in range(1, ctx_count):
        start_state = start_state + from_behind(packed_state, "ctx", distance).astype(jnp.float32)
    past = jnp.concatenate([past_kv[0], past_kv[1]], axis=1)
    half = after(half, arrived)
    w_out_halves = [
        part.reshape(group_count, head_count, -1, model_width)
        for part in (half, flip_core(half, ctx_count))
    ]
    previous = jnp.where(ctx == 0, past, arrived)
    all_keys = jnp.concatenate([previous[:, :HDIM], keys], axis=0)
    all_values = jnp.concatenate([previous[:, HDIM:], values], axis=0)
    scale = 1.0 / math.sqrt(HDIM)
    causal = jnp.arange(slab_rows)[:, None] >= jnp.arange(slab_rows)[None, :]
    offsets = jnp.arange(WINDOW + slab_rows)[None, :] - jnp.arange(slab_rows)[:, None]
    in_window = (offsets > 0) & (offsets <= WINDOW)
    carried = jnp.dot(
        query.astype(jnp.float32), start_state, precision=lax.Precision.HIGHEST
    )
    products = jnp.dot(query, all_keys.T, preferred_element_type=jnp.float32)
    inside = jnp.where(causal, products[:, WINDOW:], 0.0).astype(jnp.bfloat16)
    linear = carried + jnp.dot(inside, values, preferred_element_type=jnp.float32)
    scores = jnp.where(in_window, products * scale, -jnp.inf)
    expo = jnp.exp(scores - jnp.max(scores, axis=-1, keepdims=True))
    probs = (expo / jnp.sum(expo, axis=-1, keepdims=True)).astype(jnp.bfloat16)
    window_out = jnp.dot(probs, all_values, preferred_element_type=jnp.float32)
    heads_out = (normalize(linear) + window_out).astype(jnp.bfloat16)

    near_heads = gather_direct(jnp.concatenate([heads_out, marks], axis=0), head_count)
    far_heads = [flip_row(part, ctx_count) for part in near_heads]
    across.append(flip_row(after(blocks[-1], *far_heads), ctx_count))
    own_expert = ctx * head_count + place
    other_expert = (ctx ^ 1) * head_count + place

    across[2] = after(across[2], across[-1])
    group = lax.axis_index("groups")
    slots = [
        ((ctx % 2) ^ side) * group_count + (group ^ other)
        for side in range(2)
        for other in range(group_count)
    ]

    carry = None
    for s in list(range(1, head_count)) + [0]:
        where = jnp.stack([starts[s], own_expert, other_expert, *slots])
        near, far, *hidden = run_chunk(
            s, where, near_heads, far_heads, blocks[s], across[s], w_out_halves, experts
        )
        joined = near.astype(jnp.float32) + flip_row(far, ctx_count).astype(jnp.float32)
        if carry is not None:
            joined = joined + carry.astype(jnp.float32)
        if s:
            carry = lax.ppermute(
                joined.astype(jnp.bfloat16), "heads", ring_pairs(head_count, 1)
            )
    return (hidden[0].astype(jnp.float32) + joined).astype(jnp.bfloat16)


def solution(mesh):
    sizes = mesh.shape

    def on_device(*args):
        w_qkv, w_gate, expert_ids = args[3], args[5], args[8]
        expert_count = w_gate.shape[0] * sizes["ctx"] * sizes["heads"]
        slab_rows = args[0].shape[0] * sizes["heads"]
        dense = (
            sizes["ctx"] == 4
            and sizes["heads"] == 4
            and sizes["groups"] <= 2
            and w_gate.shape[0] == 1
            and w_qkv.shape[2] == HDIM
            and slab_rows == WINDOW
            and args[0].shape[0] == HDIM
            and expert_count % 8 == 0
            and expert_count <= 2 * expert_ids.shape[1]
        )
        return (on_device_dense if dense else on_device_routed)(*args)

    return jax.shard_map(
        on_device,
        mesh=mesh,
        in_specs=(
            P(("groups", "ctx", "heads"), None),
            P("heads", "groups", None),
            P(None, "groups", "heads"),
            P(None, None, "heads"),
            P("heads", None),
            P(("ctx", "heads"), None, None),
            P(("ctx", "heads"), None, None),
            P(("ctx", "heads"), None, None),
            P(("groups", "ctx", "heads"), None),
            P(("groups", "ctx", "heads"), None),
        ),
        out_specs=P(("groups", "ctx", "heads"), None),
        check_vma=False,
    )
```

```python
import functools
import math

import jax
import jax.numpy as jnp
from jax import lax
from jax.experimental import pallas as pl
from jax.experimental.pallas import tpu as pltpu
from jax.sharding import PartitionSpec as P

HDIM = 128
WINDOW = 512


def entering(x, axis, join, neutral):
    place = lax.axis_index(axis)
    gathered = lax.all_gather(x.astype(jnp.bfloat16), axis)
    state = jnp.zeros_like(x) + jnp.asarray(neutral, x.dtype)

    def one(lap, state):
        return join(state, lax.dynamic_index_in_dim(gathered, lap, 0, False).astype(x.dtype))

    return lax.fori_loop(0, place, one, state)


def from_behind(block, axis, distance):
    devices = range(lax.axis_size(axis))
    route = [(i - distance, i) for i in devices if i - distance in devices]
    return lax.ppermute(block, axis, route)


def normalize(value):
    return value * lax.rsqrt(jnp.mean(value * value, axis=-1, keepdims=True) + 1e-06)


def on_device_routed(
    tokens, state_in, past_kv, w_qkv, w_out, w_gate, w_up, w_down, expert_ids, gate_weights
):
    row_count, model_width = tokens.shape
    inner_width = w_qkv.shape[2]
    local_heads = inner_width // HDIM
    w_flat = w_qkv.reshape(model_width, 3 * inner_width)
    projected = jnp.dot(
        lax.all_gather(tokens, "heads", axis=0, tiled=True),
        w_flat,
        preferred_element_type=jnp.float32,
    ).astype(jnp.bfloat16)
    slab_rows = projected.shape[0]
    projected = projected.reshape(slab_rows, 3, local_heads, HDIM)
    query = jnp.transpose(projected[:, 0], (1, 0, 2))
    keys = jnp.transpose(projected[:, 1], (1, 0, 2))
    values = jnp.transpose(projected[:, 2], (1, 0, 2))
    local_state = jnp.einsum("hsd,hse->hde", keys, values, preferred_element_type=jnp.float32)
    earlier_state = entering(
        local_state, "ctx", lambda first, second: first + second, jnp.zeros_like(local_state)
    )
    start_state = state_in + earlier_state
    tail = jnp.stack([keys, values], axis=0)
    arrived = from_behind(tail, "ctx", 1)
    past = jnp.transpose(past_kv.reshape(2, WINDOW, local_heads, HDIM), (0, 2, 1, 3))
    previous = jnp.where(lax.axis_index("ctx") == 0, past, arrived)
    all_keys = jnp.concatenate([previous[0], keys], axis=1)
    all_values = jnp.concatenate([previous[1], values], axis=1)
    block_rows = min(slab_rows, 512)
    block_count = slab_rows // block_rows
    scale = 1.0 / math.sqrt(HDIM)
    causal = jnp.arange(block_rows)[:, None] >= jnp.arange(block_rows)[None, :]
    offsets = jnp.arange(WINDOW + block_rows)[None, :] - jnp.arange(block_rows)[:, None]
    in_window = (offsets > 0) & (offsets <= WINDOW)

    def block_step(state, index):
        first = index * block_rows
        carried = jnp.einsum(
            "hsd,hde->hse", query.astype(jnp.float32), state, precision=lax.Precision.HIGHEST
        )
        inside = jnp.einsum("hsd,htd->hst", query, keys, preferred_element_type=jnp.float32)
        inside = jnp.where(causal[None], inside, 0.0).astype(jnp.bfloat16)
        linear = carried + jnp.einsum(
            "hst,hte->hse", inside, values, preferred_element_type=jnp.float32
        )
        scores = (
            jnp.einsum("hsd,htd->hst", query, all_keys, preferred_element_type=jnp.float32) * scale
        )
        scores = jnp.where(in_window[None], scores, -jnp.inf)
        top_score = jnp.max(scores, axis=-1, keepdims=True)
        expo = jnp.exp(scores - top_score)
        probs = (expo / jnp.sum(expo, axis=-1, keepdims=True)).astype(jnp.bfloat16)
        window_out = jnp.einsum(
            "hst,hte->hse", probs, all_values, preferred_element_type=jnp.float32
        )
        combined = (normalize(linear) + window_out).astype(jnp.bfloat16)
        new_state = state + jnp.einsum(
            "hsd,hse->hde", keys, values, preferred_element_type=jnp.float32
        )
        return (new_state, combined)

    _, outs = lax.scan(block_step, start_state, jnp.arange(block_count, dtype=jnp.int32))
    heads_out = jnp.transpose(outs, (0, 2, 1, 3)).reshape(slab_rows, inner_width)
    regrouped = lax.all_to_all(heads_out, "heads", split_axis=0, concat_axis=1, tiled=True)
    attn = jnp.dot(
        regrouped,
        lax.all_gather(w_out, "heads", axis=0, tiled=True),
        preferred_element_type=jnp.float32,
    )
    hidden_state = (tokens.astype(jnp.float32) + attn).astype(jnp.bfloat16)
    hidden_float = hidden_state.astype(jnp.float32)
    normed = normalize(hidden_float).astype(jnp.bfloat16)
    ctx_count = lax.axis_size("ctx")
    head_count = lax.axis_size("heads")
    exp_local = w_gate.shape[0]
    expert_count = exp_local * ctx_count * head_count
    top_count = expert_ids.shape[1]
    capacity = max(2, 2 * row_count * top_count // expert_count)
    picks = expert_ids.reshape(-1)
    onehot = (picks[:, None] == jnp.arange(expert_count, dtype=jnp.int32)[None, :]).astype(
        jnp.int32
    )
    earlier = jnp.cumsum(onehot, axis=0) - onehot
    slots = jnp.sum(onehot * earlier, axis=1)
    destination = picks * capacity + slots
    source_rows = jnp.arange(row_count * top_count, dtype=jnp.int32) // top_count
    outgoing = jnp.zeros((expert_count * capacity, model_width), jnp.bfloat16)
    outgoing = outgoing.at[destination].set(normed[source_rows])
    sendable = outgoing.reshape(expert_count, 1, capacity, model_width)
    arrived_rows = lax.all_to_all(
        sendable, ("ctx", "heads"), split_axis=0, concat_axis=1, tiled=True
    )
    e_count, n_count, c_count, d_count = arrived_rows.shape
    flat = arrived_rows.reshape(e_count, n_count * c_count, d_count)
    gate_act = jnp.einsum("erd,edf->erf", flat, w_gate, preferred_element_type=jnp.float32)
    up_act = jnp.einsum("erd,edf->erf", flat, w_up, preferred_element_type=jnp.float32)
    hid = (jax.nn.silu(gate_act) * up_act).astype(jnp.bfloat16)
    out_rows = jnp.einsum("erf,efd->erd", hid, w_down, preferred_element_type=jnp.float32)
    finished = out_rows.astype(jnp.bfloat16).reshape(e_count, n_count, c_count, d_count)
    returned = lax.all_to_all(finished, ("ctx", "heads"), split_axis=1, concat_axis=0, tiled=True)
    returned = returned.reshape(expert_count * capacity, model_width)
    picked = returned[destination].reshape(row_count, top_count, model_width).astype(jnp.float32)
    routed = jnp.sum(gate_weights[:, :, None] * picked, axis=1)
    return (hidden_float + routed).astype(jnp.bfloat16)


def ring_pairs(count, step):
    return [(i, (i + step) % count) for i in range(count)]


def partner_pairs(count, bit):
    return [(i, i ^ bit) for i in range(count)]


def after(value, *others):
    return lax.optimization_barrier((value, *others))[0]


def next_place(block, count):
    return lax.ppermute(block, "heads", ring_pairs(count, 1))


def gather_direct(block, count):
    return [block] + [
        lax.ppermute(block, "heads", ring_pairs(count, step)) for step in range(1, count)
    ]


def gather_both_ways(block, count):
    parts = [block] + [None] * (count - 1)
    for step in range(1, count // 2 + 1):
        parts[step] = lax.ppermute(parts[step - 1], "heads", ring_pairs(count, 1))
        if step < count - step:
            before = parts[(1 - step) % count]
            parts[-step] = lax.ppermute(before, "heads", ring_pairs(count, -1))
    return parts


def flip_row(block, ctx_count):
    return lax.ppermute(block, "ctx", partner_pairs(ctx_count, 2))


def flip_core(block, ctx_count):
    return lax.ppermute(block, "ctx", partner_pairs(ctx_count, 1))


def w_out_piece(w_out, group_count):
    piece_rows = w_out.shape[0] // (2 * group_count)
    place = (lax.axis_index("ctx") % 2) * group_count + lax.axis_index("groups")
    return lax.dynamic_slice_in_dim(w_out, place * piece_rows, piece_rows, 0)


def chunk_kernel(head_count, turn, place_ref, *refs):
    near_heads = refs[:head_count]
    far_heads = refs[head_count : 2 * head_count]
    near_tokens, far_tokens, near_out_w, far_out_w, *weights = refs[
        2 * head_count : 2 * head_count + 10
    ]
    outs = refs[2 * head_count + 10 : -10]
    heads_buf, token_buf, mark_buf, w_out_buf, *rest = refs[-10:]
    wide_bufs, narrow_bufs, normed_buf, total_buf, small_sems, weight_sems = rest
    row_count, model_width = outs[0].shape
    slab_rows = row_count * head_count
    experts, mark_rows = narrow_bufs.shape[0], mark_buf.shape[1]
    first = pl.multiple_of(place_ref[turn], row_count)

    pairs = []
    for side, (heads_in, tokens_in) in enumerate(
        ((near_heads, near_tokens), (far_heads, far_tokens))
    ):
        rows = pl.ds(side * row_count, row_count)
        for turns in range(head_count):
            source = heads_in[turns].at[pl.ds(first, row_count)]
            pairs.append((source, heads_buf.at[rows, pl.ds(turns * HDIM, HDIM)]))
        pairs.append((tokens_in, token_buf.at[rows]))
        pairs.append((heads_in[turn].at[pl.ds(slab_rows, mark_rows)], mark_buf.at[side]))
    group_count = near_out_w.shape[0]
    for core, pieces in enumerate((near_out_w, far_out_w)):
        for group in range(group_count):
            slot = place_ref[head_count + 2 + core * group_count + group]
            pairs.append((pieces.at[group], w_out_buf.at[:, slot]))
    small = [
        pltpu.make_async_copy(source, target, small_sems.at[i])
        for i, (source, target) in enumerate(pairs)
    ]
    large = []
    for expert in range(experts):
        targets = (wide_bufs.at[expert, 0], wide_bufs.at[expert, 1], narrow_bufs.at[expert])
        for kind, target in enumerate(targets):
            copy = pltpu.make_async_copy(
                weights[3 * expert + kind].at[0], target, weight_sems.at[3 * expert + kind]
            )
            large.append(copy)

    for copy in small:
        copy.start()
    large[0].start()
    for copy in small:
        copy.wait()
    large[1].start()

    w_out_rows = w_out_buf[...].reshape(head_count * HDIM, model_width)
    attn = jnp.dot(heads_buf[...], w_out_rows, preferred_element_type=jnp.float32)
    hidden = (token_buf[...].astype(jnp.float32) + attn).astype(jnp.bfloat16)
    if len(outs) == 3:
        outs[2][...] = hidden[:row_count]
    normed_buf[...] = normalize(hidden.astype(jnp.float32)).astype(jnp.bfloat16)

    spots = lax.rem(lax.broadcasted_iota(jnp.int32, (mark_rows, HDIM), 0), mark_rows // 2)
    for expert in range(experts):
        chosen = jnp.where(spots == place_ref[head_count + expert], 1.0, 0.0).astype(jnp.bfloat16)
        gating = jnp.concatenate(
            [
                lax.dot_general(
                    mark_buf[side],
                    chosen,
                    (((0,), (0,)), ((), ())),
                    preferred_element_type=jnp.float32,
                )[:, :1]
                for side in range(2)
            ],
            axis=0,
        )
        acts = []
        for kind in range(3):
            step = 3 * expert + kind
            if step + 2 < len(large):
                large[step + 2].start()
            large[step].wait()
            if kind < 2:
                acts.append(
                    jnp.dot(
                        normed_buf[...], wide_bufs[expert, kind], preferred_element_type=jnp.float32
                    )
                )
        hid = (jax.nn.silu(acts[0]) * acts[1]).astype(jnp.bfloat16)
        rows = jnp.dot(hid, narrow_bufs[expert], preferred_element_type=jnp.float32)
        rows = rows.astype(jnp.bfloat16).astype(jnp.float32) * gating
        if expert:
            rows = rows + total_buf[...]
        if expert < experts - 1:
            total_buf[...] = rows
        else:
            rows = rows.astype(jnp.bfloat16)
            outs[0][...] = rows[:row_count]
            outs[1][...] = rows[row_count:]


def run_chunk(turn, place, near_heads, far_heads, near_tokens, far_tokens, w_out, weights):
    row_count, model_width = near_tokens.shape
    head_count = len(near_heads)
    inner = weights[0].shape[2]
    rows = 2 * row_count
    mark_rows = near_heads[0].shape[0] - row_count * head_count
    experts = len(weights) // 3
    outs = 2 if turn else 3
    anywhere = pl.BlockSpec(memory_space=pl.ANY)
    operands = [*near_heads, *far_heads, near_tokens, far_tokens, *w_out, *weights]
    group_count, _, piece_rows, _ = w_out[0].shape
    flops = 2 * rows * model_width * (3 * experts * inner + head_count * HDIM)
    return pl.pallas_call(
        functools.partial(chunk_kernel, head_count, turn),
        out_shape=[jax.ShapeDtypeStruct((row_count, model_width), jnp.bfloat16)] * outs,
        in_specs=[pl.BlockSpec(memory_space=pltpu.SMEM)] + [anywhere] * len(operands),
        out_specs=[pl.BlockSpec(memory_space=pltpu.VMEM)] * outs,
        scratch_shapes=[
            pltpu.VMEM((rows, head_count * HDIM), jnp.bfloat16),
            pltpu.VMEM((rows, model_width), jnp.bfloat16),
            pltpu.VMEM((2, mark_rows, row_count), jnp.bfloat16),
            pltpu.VMEM((head_count, 2 * group_count, piece_rows, model_width), jnp.bfloat16),
            pltpu.VMEM((experts, 2, model_width, inner), jnp.bfloat16),
            pltpu.VMEM((experts, inner, model_width), jnp.bfloat16),
            pltpu.VMEM((rows, model_width), jnp.bfloat16),
            pltpu.VMEM((rows, model_width), jnp.float32),
            pltpu.SemaphoreType.DMA((2 * (head_count + 2 + group_count),)),
            pltpu.SemaphoreType.DMA((3 * experts,)),
        ],
        compiler_params=pltpu.CompilerParams(vmem_limit_bytes=60 * 2**20),
        cost_estimate=pl.CostEstimate(
            flops=flops, bytes_accessed=sum(2 * math.prod(w.shape) for w in weights), transcendentals=0
        ),
        name="chunk",
    )(place, *operands)


def on_device_dense(
    tokens, state_in, past_kv, w_qkv, w_out, w_gate, w_up, w_down, expert_ids, gate_weights
):
    row_count, model_width = tokens.shape
    head_count = lax.axis_size("heads")
    ctx_count = lax.axis_size("ctx")
    group_count = lax.axis_size("groups")
    ctx = lax.axis_index("ctx")
    place = lax.axis_index("heads")
    slab_rows = row_count * head_count
    expert_count = ctx_count * head_count
    starts = [((place - s) % head_count) * row_count for s in range(head_count)]

    hit = expert_ids[:, :, None] == jnp.arange(expert_count, dtype=jnp.int32)[None, None, :]
    dense_weights = jnp.sum(jnp.where(hit, gate_weights[:, :, None], 0.0), axis=1)
    coarse = lax.reduce_precision(dense_weights, 8, 7)
    halves = [coarse, dense_weights - coarse]
    marks = jnp.concatenate(halves, axis=1).astype(jnp.bfloat16).T

    w_flat = w_qkv.reshape(model_width, 3 * HDIM)
    projected = jnp.zeros((slab_rows, 3 * HDIM), jnp.bfloat16)

    def project(projected, s):
        part = jnp.dot(blocks[s], w_flat, preferred_element_type=jnp.float32)
        return lax.dynamic_update_slice_in_dim(projected, part.astype(jnp.bfloat16), starts[s], 0)

    own_expert = ctx * head_count + place
    other_expert = (ctx ^ 1) * head_count + place

    group = lax.axis_index("groups")
    slots = [
        ((ctx % 2) ^ side) * group_count + (group ^ other)
        for side in range(2)
        for other in range(group_count)
    ]
    where = jnp.stack([*starts, own_expert, other_expert, *slots])
    experts = [w_gate, w_up, w_down]
    blocks, across, swapped = [tokens], [], []
    pieces = [w_out_piece(w_out, group_count)] + [None] * (head_count - 1)
    for s in range(head_count - 1):
        blocks.append(next_place(blocks[s], head_count))
        across.append(flip_row(blocks[s], ctx_count))
        swapped.append(flip_core(after(experts[s], blocks[s]), ctx_count))
        projected = project(projected, s)
        for distance in ((1, head_count - 1), range(2, head_count - 1), ())[s]:
            piece = after(pieces[0], blocks[s], swapped[s])
            pieces[distance] = lax.ppermute(piece, "heads", ring_pairs(head_count, distance))
        extra = (pieces, halves)[s - 1] if s else []
        blocks[-1], across[-1], swapped[-1], projected, where, *extra = lax.optimization_barrier(
            (blocks[-1], across[-1], swapped[-1], projected, where, *extra)
        )
        if s == 1:
            halves = [jnp.concatenate(extra, axis=0)]
            if group_count == 2:
                halves.append(lax.ppermute(halves[0], "groups", [(0, 1), (1, 0)]))
    half = jnp.stack(extra, axis=0)
    projected = project(projected, head_count - 1)
    experts = experts + swapped

    query = projected[:, :HDIM]
    keys = projected[:, HDIM : 2 * HDIM]
    values = projected[:, 2 * HDIM :]
    local_state = jnp.dot(keys.T, values, preferred_element_type=jnp.float32)
    arrived = from_behind(projected[:, HDIM:], "ctx", 1)
    start_state = state_in[0]
    packed_state = local_state.astype(jnp.bfloat16)
    for distance in range(2, ctx_count):
        start_state = start_state + from_behind(packed_state, "ctx", distance).astype(jnp.float32)
    start_state = start_state + jnp.dot(
        arrived[:, :HDIM].T, arrived[:, HDIM:], preferred_element_type=jnp.float32
    )
    past = jnp.concatenate([past_kv[0], past_kv[1]], axis=1)
    half = after(half, arrived)
    w_out_halves = [
        part.reshape(group_count, head_count, -1, model_width)
        for part in (half, flip_core(half, ctx_count))
    ]
    previous = jnp.where(ctx == 0, past, arrived)
    all_keys = jnp.concatenate([previous[:, :HDIM], keys], axis=0)
    all_values = jnp.concatenate([previous[:, HDIM:], values], axis=0)
    scale = 1.0 / math.sqrt(HDIM)
    causal = jnp.arange(slab_rows)[:, None] >= jnp.arange(slab_rows)[None, :]
    offsets = jnp.arange(WINDOW + slab_rows)[None, :] - jnp.arange(slab_rows)[:, None]
    in_window = (offsets > 0) & (offsets <= WINDOW)
    carried = jnp.dot(
        query.astype(jnp.float32), start_state, precision=lax.Precision.HIGHEST
    )
    products = jnp.dot(query, all_keys.T, preferred_element_type=jnp.float32)
    inside = jnp.where(causal, products[:, WINDOW:], 0.0).astype(jnp.bfloat16)
    linear = carried + jnp.dot(inside, values, preferred_element_type=jnp.float32)
    scores = jnp.where(in_window, products * scale, -jnp.inf)
    expo = jnp.exp(scores - jnp.max(scores, axis=-1, keepdims=True))
    probs = (expo / jnp.sum(expo, axis=-1, keepdims=True)).astype(jnp.bfloat16)
    window_out = jnp.dot(probs, all_values, preferred_element_type=jnp.float32)
    heads_out = (normalize(linear) + window_out).astype(jnp.bfloat16)

    near_heads = gather_direct(jnp.concatenate([heads_out, marks], axis=0), head_count)
    far_heads = [flip_row(part, ctx_count) for part in near_heads]
    across.append(flip_row(after(blocks[-1], *far_heads), ctx_count))
    across[2] = after(across[2], across[-1])
    carry = None
    for s in list(range(1, head_count)) + [0]:
        near, far, *hidden = run_chunk(
            s, where, near_heads, far_heads, blocks[s], across[s], w_out_halves, experts
        )
        joined = near.astype(jnp.float32) + flip_row(far, ctx_count).astype(jnp.float32)
        if carry is not None:
            joined = joined + carry.astype(jnp.float32)
        if s:
            carry = lax.ppermute(
                joined.astype(jnp.bfloat16), "heads", ring_pairs(head_count, 1)
            )
    return (hidden[0].astype(jnp.float32) + joined).astype(jnp.bfloat16)


def solution(mesh):
    sizes = mesh.shape

    def on_device(*args):
        w_qkv, w_gate, expert_ids = args[3], args[5], args[8]
        expert_count = w_gate.shape[0] * sizes["ctx"] * sizes["heads"]
        slab_rows = args[0].shape[0] * sizes["heads"]
        dense = (
            sizes["ctx"] == 4
            and sizes["heads"] == 4
            and sizes["groups"] <= 2
            and w_gate.shape[0] == 1
            and w_qkv.shape[2] == HDIM
            and slab_rows == WINDOW
            and args[0].shape[0] == HDIM
            and expert_count % 8 == 0
            and expert_count <= 2 * expert_ids.shape[1]
        )
        return (on_device_dense if dense else on_device_routed)(*args)

    return jax.shard_map(
        on_device,
        mesh=mesh,
        in_specs=(
            P(("groups", "ctx", "heads"), None),
            P("heads", "groups", None),
            P(None, "groups", "heads"),
            P(None, None, "heads"),
            P("heads", None),
            P(("ctx", "heads"), None, None),
            P(("ctx", "heads"), None, None),
            P(("ctx", "heads"), None, None),
            P(("groups", "ctx", "heads"), None),
            P(("groups", "ctx", "heads"), None),
        ),
        out_specs=P(("groups", "ctx", "heads"), None),
        check_vma=False,
    )
```

```python
import functools
import math

import jax
import jax.numpy as jnp
from jax import lax
from jax.experimental import pallas as pl
from jax.experimental.pallas import tpu as pltpu
from jax.sharding import PartitionSpec as P

HDIM = 128
WINDOW = 512


def entering(x, axis, join, neutral):
    place = lax.axis_index(axis)
    gathered = lax.all_gather(x.astype(jnp.bfloat16), axis)
    state = jnp.zeros_like(x) + jnp.asarray(neutral, x.dtype)

    def one(lap, state):
        return join(state, lax.dynamic_index_in_dim(gathered, lap, 0, False).astype(x.dtype))

    return lax.fori_loop(0, place, one, state)


def from_behind(block, axis, distance):
    devices = range(lax.axis_size(axis))
    route = [(i - distance, i) for i in devices if i - distance in devices]
    return lax.ppermute(block, axis, route)


def normalize(value):
    return value * lax.rsqrt(jnp.mean(value * value, axis=-1, keepdims=True) + 1e-06)


def on_device_routed(
    tokens, state_in, past_kv, w_qkv, w_out, w_gate, w_up, w_down, expert_ids, gate_weights
):
    row_count, model_width = tokens.shape
    inner_width = w_qkv.shape[2]
    local_heads = inner_width // HDIM
    w_flat = w_qkv.reshape(model_width, 3 * inner_width)
    projected = jnp.dot(
        lax.all_gather(tokens, "heads", axis=0, tiled=True),
        w_flat,
        preferred_element_type=jnp.float32,
    ).astype(jnp.bfloat16)
    slab_rows = projected.shape[0]
    projected = projected.reshape(slab_rows, 3, local_heads, HDIM)
    query = jnp.transpose(projected[:, 0], (1, 0, 2))
    keys = jnp.transpose(projected[:, 1], (1, 0, 2))
    values = jnp.transpose(projected[:, 2], (1, 0, 2))
    local_state = jnp.einsum("hsd,hse->hde", keys, values, preferred_element_type=jnp.float32)
    earlier_state = entering(
        local_state, "ctx", lambda first, second: first + second, jnp.zeros_like(local_state)
    )
    start_state = state_in + earlier_state
    tail = jnp.stack([keys, values], axis=0)
    arrived = from_behind(tail, "ctx", 1)
    past = jnp.transpose(past_kv.reshape(2, WINDOW, local_heads, HDIM), (0, 2, 1, 3))
    previous = jnp.where(lax.axis_index("ctx") == 0, past, arrived)
    all_keys = jnp.concatenate([previous[0], keys], axis=1)
    all_values = jnp.concatenate([previous[1], values], axis=1)
    block_rows = min(slab_rows, 512)
    block_count = slab_rows // block_rows
    scale = 1.0 / math.sqrt(HDIM)
    causal = jnp.arange(block_rows)[:, None] >= jnp.arange(block_rows)[None, :]
    offsets = jnp.arange(WINDOW + block_rows)[None, :] - jnp.arange(block_rows)[:, None]
    in_window = (offsets > 0) & (offsets <= WINDOW)

    def block_step(state, index):
        first = index * block_rows
        carried = jnp.einsum(
            "hsd,hde->hse", query.astype(jnp.float32), state, precision=lax.Precision.HIGHEST
        )
        inside = jnp.einsum("hsd,htd->hst", query, keys, preferred_element_type=jnp.float32)
        inside = jnp.where(causal[None], inside, 0.0).astype(jnp.bfloat16)
        linear = carried + jnp.einsum(
            "hst,hte->hse", inside, values, preferred_element_type=jnp.float32
        )
        scores = (
            jnp.einsum("hsd,htd->hst", query, all_keys, preferred_element_type=jnp.float32) * scale
        )
        scores = jnp.where(in_window[None], scores, -jnp.inf)
        top_score = jnp.max(scores, axis=-1, keepdims=True)
        expo = jnp.exp(scores - top_score)
        probs = (expo / jnp.sum(expo, axis=-1, keepdims=True)).astype(jnp.bfloat16)
        window_out = jnp.einsum(
            "hst,hte->hse", probs, all_values, preferred_element_type=jnp.float32
        )
        combined = (normalize(linear) + window_out).astype(jnp.bfloat16)
        new_state = state + jnp.einsum(
            "hsd,hse->hde", keys, values, preferred_element_type=jnp.float32
        )
        return (new_state, combined)

    _, outs = lax.scan(block_step, start_state, jnp.arange(block_count, dtype=jnp.int32))
    heads_out = jnp.transpose(outs, (0, 2, 1, 3)).reshape(slab_rows, inner_width)
    regrouped = lax.all_to_all(heads_out, "heads", split_axis=0, concat_axis=1, tiled=True)
    attn = jnp.dot(
        regrouped,
        lax.all_gather(w_out, "heads", axis=0, tiled=True),
        preferred_element_type=jnp.float32,
    )
    hidden_state = (tokens.astype(jnp.float32) + attn).astype(jnp.bfloat16)
    hidden_float = hidden_state.astype(jnp.float32)
    normed = normalize(hidden_float).astype(jnp.bfloat16)
    ctx_count = lax.axis_size("ctx")
    head_count = lax.axis_size("heads")
    exp_local = w_gate.shape[0]
    expert_count = exp_local * ctx_count * head_count
    top_count = expert_ids.shape[1]
    capacity = max(2, 2 * row_count * top_count // expert_count)
    picks = expert_ids.reshape(-1)
    onehot = (picks[:, None] == jnp.arange(expert_count, dtype=jnp.int32)[None, :]).astype(
        jnp.int32
    )
    earlier = jnp.cumsum(onehot, axis=0) - onehot
    slots = jnp.sum(onehot * earlier, axis=1)
    destination = picks * capacity + slots
    source_rows = jnp.arange(row_count * top_count, dtype=jnp.int32) // top_count
    outgoing = jnp.zeros((expert_count * capacity, model_width), jnp.bfloat16)
    outgoing = outgoing.at[destination].set(normed[source_rows])
    sendable = outgoing.reshape(expert_count, 1, capacity, model_width)
    arrived_rows = lax.all_to_all(
        sendable, ("ctx", "heads"), split_axis=0, concat_axis=1, tiled=True
    )
    e_count, n_count, c_count, d_count = arrived_rows.shape
    flat = arrived_rows.reshape(e_count, n_count * c_count, d_count)
    gate_act = jnp.einsum("erd,edf->erf", flat, w_gate, preferred_element_type=jnp.float32)
    up_act = jnp.einsum("erd,edf->erf", flat, w_up, preferred_element_type=jnp.float32)
    hid = (jax.nn.silu(gate_act) * up_act).astype(jnp.bfloat16)
    out_rows = jnp.einsum("erf,efd->erd", hid, w_down, preferred_element_type=jnp.float32)
    finished = out_rows.astype(jnp.bfloat16).reshape(e_count, n_count, c_count, d_count)
    returned = lax.all_to_all(finished, ("ctx", "heads"), split_axis=1, concat_axis=0, tiled=True)
    returned = returned.reshape(expert_count * capacity, model_width)
    picked = returned[destination].reshape(row_count, top_count, model_width).astype(jnp.float32)
    routed = jnp.sum(gate_weights[:, :, None] * picked, axis=1)
    return (hidden_float + routed).astype(jnp.bfloat16)


def ring_pairs(count, step):
    return [(i, (i + step) % count) for i in range(count)]


def partner_pairs(count, bit):
    return [(i, i ^ bit) for i in range(count)]


def after(value, *others):
    return lax.optimization_barrier((value, *others))[0]


def next_place(block, count):
    return lax.ppermute(block, "heads", ring_pairs(count, 1))


def gather_direct(block, count):
    return [block] + [
        lax.ppermute(block, "heads", ring_pairs(count, step)) for step in range(1, count)
    ]


def gather_both_ways(block, count):
    parts = [block] + [None] * (count - 1)
    for step in range(1, count // 2 + 1):
        parts[step] = lax.ppermute(parts[step - 1], "heads", ring_pairs(count, 1))
        if step < count - step:
            before = parts[(1 - step) % count]
            parts[-step] = lax.ppermute(before, "heads", ring_pairs(count, -1))
    return parts


def flip_row(block, ctx_count):
    return lax.ppermute(block, "ctx", partner_pairs(ctx_count, 2))


def flip_core(block, ctx_count):
    return lax.ppermute(block, "ctx", partner_pairs(ctx_count, 1))


def w_out_piece(w_out, group_count):
    piece_rows = w_out.shape[0] // (2 * group_count)
    place = (lax.axis_index("ctx") % 2) * group_count + lax.axis_index("groups")
    return lax.dynamic_slice_in_dim(w_out, place * piece_rows, piece_rows, 0)


def chunk_kernel(head_count, turn, place_ref, *refs):
    near_heads = refs[:head_count]
    far_heads = refs[head_count : 2 * head_count]
    near_tokens, far_tokens, near_out_w, far_out_w, *weights = refs[
        2 * head_count : 2 * head_count + 10
    ]
    outs = refs[2 * head_count + 10 : -10]
    heads_buf, token_buf, mark_buf, w_out_buf, *rest = refs[-10:]
    wide_bufs, narrow_bufs, normed_buf, total_buf, small_sems, weight_sems = rest
    row_count, model_width = outs[0].shape
    slab_rows = row_count * head_count
    experts, mark_rows = narrow_bufs.shape[0], mark_buf.shape[1]
    first = pl.multiple_of(place_ref[turn], row_count)

    pairs = []
    for side, (heads_in, tokens_in) in enumerate(
        ((near_heads, near_tokens), (far_heads, far_tokens))
    ):
        rows = pl.ds(side * row_count, row_count)
        for turns in range(head_count):
            source = heads_in[turns].at[pl.ds(first, row_count)]
            pairs.append((source, heads_buf.at[rows, pl.ds(turns * HDIM, HDIM)]))
        pairs.append((tokens_in, token_buf.at[rows]))
        pairs.append((heads_in[turn].at[pl.ds(slab_rows, mark_rows)], mark_buf.at[side]))
    group_count = near_out_w.shape[0]
    for core, pieces in enumerate((near_out_w, far_out_w)):
        for group in range(group_count):
            slot = place_ref[head_count + 2 + core * group_count + group]
            pairs.append((pieces.at[group], w_out_buf.at[:, slot]))
    small = [
        pltpu.make_async_copy(source, target, small_sems.at[i])
        for i, (source, target) in enumerate(pairs)
    ]
    large = []
    for expert in range(experts):
        targets = (wide_bufs.at[expert, 0], wide_bufs.at[expert, 1], narrow_bufs.at[expert])
        for kind, target in enumerate(targets):
            copy = pltpu.make_async_copy(
                weights[3 * expert + kind].at[0], target, weight_sems.at[3 * expert + kind]
            )
            large.append(copy)

    for copy in small:
        copy.start()
    large[0].start()
    for copy in small:
        copy.wait()
    large[1].start()

    w_out_rows = w_out_buf[...].reshape(head_count * HDIM, model_width)
    attn = jnp.dot(heads_buf[...], w_out_rows, preferred_element_type=jnp.float32)
    hidden = (token_buf[...].astype(jnp.float32) + attn).astype(jnp.bfloat16)
    if len(outs) == 3:
        outs[2][...] = hidden[:row_count]
    normed_buf[...] = normalize(hidden.astype(jnp.float32)).astype(jnp.bfloat16)

    spots = lax.rem(lax.broadcasted_iota(jnp.int32, (mark_rows, HDIM), 0), mark_rows // 2)
    for expert in range(experts):
        chosen = jnp.where(spots == place_ref[head_count + expert], 1.0, 0.0).astype(jnp.bfloat16)
        gating = jnp.concatenate(
            [
                lax.dot_general(
                    mark_buf[side],
                    chosen,
                    (((0,), (0,)), ((), ())),
                    preferred_element_type=jnp.float32,
                )[:, :1]
                for side in range(2)
            ],
            axis=0,
        )
        acts = []
        for kind in range(3):
            step = 3 * expert + kind
            if step + 2 < len(large):
                large[step + 2].start()
            large[step].wait()
            if kind < 2:
                acts.append(
                    jnp.dot(
                        normed_buf[...], wide_bufs[expert, kind], preferred_element_type=jnp.float32
                    )
                )
        hid = (jax.nn.silu(acts[0]) * acts[1]).astype(jnp.bfloat16)
        rows = jnp.dot(hid, narrow_bufs[expert], preferred_element_type=jnp.float32)
        rows = rows.astype(jnp.bfloat16).astype(jnp.float32) * gating
        if expert:
            rows = rows + total_buf[...]
        if expert < experts - 1:
            total_buf[...] = rows
        else:
            rows = rows.astype(jnp.bfloat16)
            outs[0][...] = rows[:row_count]
            outs[1][...] = rows[row_count:]


def run_chunk(turn, place, near_heads, far_heads, near_tokens, far_tokens, w_out, weights):
    row_count, model_width = near_tokens.shape
    head_count = len(near_heads)
    inner = weights[0].shape[2]
    rows = 2 * row_count
    mark_rows = near_heads[0].shape[0] - row_count * head_count
    experts = len(weights) // 3
    outs = 2 if turn else 3
    anywhere = pl.BlockSpec(memory_space=pl.ANY)
    operands = [*near_heads, *far_heads, near_tokens, far_tokens, *w_out, *weights]
    group_count, _, piece_rows, _ = w_out[0].shape
    flops = 2 * rows * model_width * (3 * experts * inner + head_count * HDIM)
    return pl.pallas_call(
        functools.partial(chunk_kernel, head_count, turn),
        out_shape=[jax.ShapeDtypeStruct((row_count, model_width), jnp.bfloat16)] * outs,
        in_specs=[pl.BlockSpec(memory_space=pltpu.SMEM)] + [anywhere] * len(operands),
        out_specs=[pl.BlockSpec(memory_space=pltpu.VMEM)] * outs,
        scratch_shapes=[
            pltpu.VMEM((rows, head_count * HDIM), jnp.bfloat16),
            pltpu.VMEM((rows, model_width), jnp.bfloat16),
            pltpu.VMEM((2, mark_rows, row_count), jnp.bfloat16),
            pltpu.VMEM((head_count, 2 * group_count, piece_rows, model_width), jnp.bfloat16),
            pltpu.VMEM((experts, 2, model_width, inner), jnp.bfloat16),
            pltpu.VMEM((experts, inner, model_width), jnp.bfloat16),
            pltpu.VMEM((rows, model_width), jnp.bfloat16),
            pltpu.VMEM((rows, model_width), jnp.float32),
            pltpu.SemaphoreType.DMA((2 * (head_count + 2 + group_count),)),
            pltpu.SemaphoreType.DMA((3 * experts,)),
        ],
        compiler_params=pltpu.CompilerParams(vmem_limit_bytes=61 * 2**20),
        cost_estimate=pl.CostEstimate(
            flops=flops, bytes_accessed=sum(2 * math.prod(w.shape) for w in weights), transcendentals=0
        ),
        name="chunk",
    )(place, *operands)


def on_device_dense(
    tokens, state_in, past_kv, w_qkv, w_out, w_gate, w_up, w_down, expert_ids, gate_weights
):
    row_count, model_width = tokens.shape
    head_count = lax.axis_size("heads")
    ctx_count = lax.axis_size("ctx")
    group_count = lax.axis_size("groups")
    ctx = lax.axis_index("ctx")
    place = lax.axis_index("heads")
    slab_rows = row_count * head_count
    expert_count = ctx_count * head_count
    starts = [((place - s) % head_count) * row_count for s in range(head_count)]

    hit = expert_ids[:, :, None] == jnp.arange(expert_count, dtype=jnp.int32)[None, None, :]
    dense_weights = jnp.sum(jnp.where(hit, gate_weights[:, :, None], 0.0), axis=1)
    coarse = lax.reduce_precision(dense_weights, 8, 7)
    halves = [coarse, dense_weights - coarse]
    marks = jnp.concatenate(halves, axis=1).astype(jnp.bfloat16).T

    w_flat = w_qkv.reshape(model_width, 3 * HDIM)
    projected = jnp.zeros((slab_rows, 3 * HDIM), jnp.bfloat16)

    def project(projected, s):
        part = jnp.dot(blocks[s], w_flat, preferred_element_type=jnp.float32)
        return lax.dynamic_update_slice_in_dim(projected, part.astype(jnp.bfloat16), starts[s], 0)

    own_expert = ctx * head_count + place
    other_expert = (ctx ^ 1) * head_count + place

    group = lax.axis_index("groups")
    slots = [
        ((ctx % 2) ^ side) * group_count + (group ^ other)
        for side in range(2)
        for other in range(group_count)
    ]
    where = jnp.stack([*starts, own_expert, other_expert, *slots])
    experts = [w_gate, w_up, w_down]
    blocks, across, swapped = [tokens], [], []
    pieces = [w_out_piece(w_out, group_count)] + [None] * (head_count - 1)
    for s in range(head_count - 1):
        blocks.append(next_place(blocks[s], head_count))
        across.append(flip_row(blocks[s], ctx_count))
        swapped.append(flip_core(after(experts[s], blocks[s]), ctx_count))
        projected = project(projected, s)
        for distance in ((1, head_count - 1), range(2, head_count - 1), ())[s]:
            piece = after(pieces[0], blocks[s], swapped[s])
            pieces[distance] = lax.ppermute(piece, "heads", ring_pairs(head_count, distance))
        extra = pieces if s == 1 else []
        blocks[-1], across[-1], swapped[-1], projected, where, *extra = lax.optimization_barrier(
            (blocks[-1], across[-1], swapped[-1], projected, where, *extra)
        )
        if s == 1:
            halves = [jnp.concatenate(extra, axis=0)]
            if group_count == 2:
                halves.append(lax.ppermute(halves[0], "groups", [(0, 1), (1, 0)]))
    half = jnp.stack(halves, axis=0)
    projected = project(projected, head_count - 1)
    experts = experts + swapped

    query = projected[:, :HDIM]
    keys = projected[:, HDIM : 2 * HDIM]
    values = projected[:, 2 * HDIM :]
    local_state = jnp.dot(keys.T, values, preferred_element_type=jnp.float32)
    arrived = from_behind(projected[:, HDIM:], "ctx", 1)
    start_state = state_in[0]
    packed_state = local_state.astype(jnp.bfloat16)
    for distance in range(2, ctx_count):
        start_state = start_state + from_behind(packed_state, "ctx", distance).astype(jnp.float32)
    start_state = start_state + jnp.dot(
        arrived[:, :HDIM].T, arrived[:, HDIM:], preferred_element_type=jnp.float32
    )
    past = jnp.concatenate([past_kv[0], past_kv[1]], axis=1)
    half = after(half, arrived)
    w_out_halves = [
        part.reshape(group_count, head_count, -1, model_width)
        for part in (half, flip_core(half, ctx_count))
    ]
    previous = jnp.where(ctx == 0, past, arrived)
    all_keys = jnp.concatenate([previous[:, :HDIM], keys], axis=0)
    all_values = jnp.concatenate([previous[:, HDIM:], values], axis=0)
    scale = 1.0 / math.sqrt(HDIM)
    causal = jnp.arange(slab_rows)[:, None] >= jnp.arange(slab_rows)[None, :]
    offsets = jnp.arange(WINDOW + slab_rows)[None, :] - jnp.arange(slab_rows)[:, None]
    in_window = (offsets > 0) & (offsets <= WINDOW)
    carried = jnp.dot(
        query.astype(jnp.float32), start_state, precision=lax.Precision.HIGHEST
    )
    products = jnp.dot(query, all_keys.T, preferred_element_type=jnp.float32)
    inside = jnp.where(causal, products[:, WINDOW:], 0.0).astype(jnp.bfloat16)
    linear = carried + jnp.dot(inside, values, preferred_element_type=jnp.float32)
    scores = jnp.where(in_window, products * scale, -jnp.inf)
    expo = jnp.exp(scores - jnp.max(scores, axis=-1, keepdims=True))
    probs = (expo / jnp.sum(expo, axis=-1, keepdims=True)).astype(jnp.bfloat16)
    window_out = jnp.dot(probs, all_values, preferred_element_type=jnp.float32)
    heads_out = (normalize(linear) + window_out).astype(jnp.bfloat16)

    near_heads = gather_direct(jnp.concatenate([heads_out, marks], axis=0), head_count)
    far_heads = [flip_row(part, ctx_count) for part in near_heads]
    across.append(flip_row(after(blocks[-1], *far_heads), ctx_count))
    across[2] = after(across[2], across[-1])
    carry = None
    for s in list(range(1, head_count)) + [0]:
        near, far, *hidden = run_chunk(
            s, where, near_heads, far_heads, blocks[s], across[s], w_out_halves, experts
        )
        joined = near.astype(jnp.float32) + flip_row(far, ctx_count).astype(jnp.float32)
        if carry is not None:
            joined = joined + carry.astype(jnp.float32)
        if s:
            carry = lax.ppermute(
                joined.astype(jnp.bfloat16), "heads", ring_pairs(head_count, 1)
            )
    return (hidden[0].astype(jnp.float32) + joined).astype(jnp.bfloat16)


def solution(mesh):
    sizes = mesh.shape

    def on_device(*args):
        w_qkv, w_gate, expert_ids = args[3], args[5], args[8]
        expert_count = w_gate.shape[0] * sizes["ctx"] * sizes["heads"]
        slab_rows = args[0].shape[0] * sizes["heads"]
        dense = (
            sizes["ctx"] == 4
            and sizes["heads"] == 4
            and sizes["groups"] <= 2
            and w_gate.shape[0] == 1
            and w_qkv.shape[2] == HDIM
            and slab_rows == WINDOW
            and args[0].shape[0] == HDIM
            and expert_count % 8 == 0
            and expert_count <= 2 * expert_ids.shape[1]
        )
        return (on_device_dense if dense else on_device_routed)(*args)

    return jax.shard_map(
        on_device,
        mesh=mesh,
        in_specs=(
            P(("groups", "ctx", "heads"), None),
            P("heads", "groups", None),
            P(None, "groups", "heads"),
            P(None, None, "heads"),
            P("heads", None),
            P(("ctx", "heads"), None, None),
            P(("ctx", "heads"), None, None),
            P(("ctx", "heads"), None, None),
            P(("groups", "ctx", "heads"), None),
            P(("groups", "ctx", "heads"), None),
        ),
        out_specs=P(("groups", "ctx", "heads"), None),
        check_vma=False,
    )
```

```python
import functools
import math

import jax
import jax.numpy as jnp
from jax import lax
from jax.experimental import pallas as pl
from jax.experimental.pallas import tpu as pltpu
from jax.sharding import PartitionSpec as P

HDIM = 128
WINDOW = 512


def entering(x, axis, join, neutral):
    place = lax.axis_index(axis)
    gathered = lax.all_gather(x.astype(jnp.bfloat16), axis)
    state = jnp.zeros_like(x) + jnp.asarray(neutral, x.dtype)

    def one(lap, state):
        return join(state, lax.dynamic_index_in_dim(gathered, lap, 0, False).astype(x.dtype))

    return lax.fori_loop(0, place, one, state)


def from_behind(block, axis, distance):
    devices = range(lax.axis_size(axis))
    route = [(i - distance, i) for i in devices if i - distance in devices]
    return lax.ppermute(block, axis, route)


def normalize(value):
    return value * lax.rsqrt(jnp.mean(value * value, axis=-1, keepdims=True) + 1e-06)


def on_device_routed(
    tokens, state_in, past_kv, w_qkv, w_out, w_gate, w_up, w_down, expert_ids, gate_weights
):
    row_count, model_width = tokens.shape
    inner_width = w_qkv.shape[2]
    local_heads = inner_width // HDIM
    w_flat = w_qkv.reshape(model_width, 3 * inner_width)
    projected = jnp.dot(
        lax.all_gather(tokens, "heads", axis=0, tiled=True),
        w_flat,
        preferred_element_type=jnp.float32,
    ).astype(jnp.bfloat16)
    slab_rows = projected.shape[0]
    projected = projected.reshape(slab_rows, 3, local_heads, HDIM)
    query = jnp.transpose(projected[:, 0], (1, 0, 2))
    keys = jnp.transpose(projected[:, 1], (1, 0, 2))
    values = jnp.transpose(projected[:, 2], (1, 0, 2))
    local_state = jnp.einsum("hsd,hse->hde", keys, values, preferred_element_type=jnp.float32)
    earlier_state = entering(
        local_state, "ctx", lambda first, second: first + second, jnp.zeros_like(local_state)
    )
    start_state = state_in + earlier_state
    tail = jnp.stack([keys, values], axis=0)
    arrived = from_behind(tail, "ctx", 1)
    past = jnp.transpose(past_kv.reshape(2, WINDOW, local_heads, HDIM), (0, 2, 1, 3))
    previous = jnp.where(lax.axis_index("ctx") == 0, past, arrived)
    all_keys = jnp.concatenate([previous[0], keys], axis=1)
    all_values = jnp.concatenate([previous[1], values], axis=1)
    block_rows = min(slab_rows, 512)
    block_count = slab_rows // block_rows
    scale = 1.0 / math.sqrt(HDIM)
    causal = jnp.arange(block_rows)[:, None] >= jnp.arange(block_rows)[None, :]
    offsets = jnp.arange(WINDOW + block_rows)[None, :] - jnp.arange(block_rows)[:, None]
    in_window = (offsets > 0) & (offsets <= WINDOW)

    def block_step(state, index):
        first = index * block_rows
        carried = jnp.einsum(
            "hsd,hde->hse", query.astype(jnp.float32), state, precision=lax.Precision.HIGHEST
        )
        inside = jnp.einsum("hsd,htd->hst", query, keys, preferred_element_type=jnp.float32)
        inside = jnp.where(causal[None], inside, 0.0).astype(jnp.bfloat16)
        linear = carried + jnp.einsum(
            "hst,hte->hse", inside, values, preferred_element_type=jnp.float32
        )
        scores = (
            jnp.einsum("hsd,htd->hst", query, all_keys, preferred_element_type=jnp.float32) * scale
        )
        scores = jnp.where(in_window[None], scores, -jnp.inf)
        top_score = jnp.max(scores, axis=-1, keepdims=True)
        expo = jnp.exp(scores - top_score)
        probs = (expo / jnp.sum(expo, axis=-1, keepdims=True)).astype(jnp.bfloat16)
        window_out = jnp.einsum(
            "hst,hte->hse", probs, all_values, preferred_element_type=jnp.float32
        )
        combined = (normalize(linear) + window_out).astype(jnp.bfloat16)
        new_state = state + jnp.einsum(
            "hsd,hse->hde", keys, values, preferred_element_type=jnp.float32
        )
        return (new_state, combined)

    _, outs = lax.scan(block_step, start_state, jnp.arange(block_count, dtype=jnp.int32))
    heads_out = jnp.transpose(outs, (0, 2, 1, 3)).reshape(slab_rows, inner_width)
    regrouped = lax.all_to_all(heads_out, "heads", split_axis=0, concat_axis=1, tiled=True)
    attn = jnp.dot(
        regrouped,
        lax.all_gather(w_out, "heads", axis=0, tiled=True),
        preferred_element_type=jnp.float32,
    )
    hidden_state = (tokens.astype(jnp.float32) + attn).astype(jnp.bfloat16)
    hidden_float = hidden_state.astype(jnp.float32)
    normed = normalize(hidden_float).astype(jnp.bfloat16)
    ctx_count = lax.axis_size("ctx")
    head_count = lax.axis_size("heads")
    exp_local = w_gate.shape[0]
    expert_count = exp_local * ctx_count * head_count
    top_count = expert_ids.shape[1]
    capacity = max(2, 2 * row_count * top_count // expert_count)
    picks = expert_ids.reshape(-1)
    onehot = (picks[:, None] == jnp.arange(expert_count, dtype=jnp.int32)[None, :]).astype(
        jnp.int32
    )
    earlier = jnp.cumsum(onehot, axis=0) - onehot
    slots = jnp.sum(onehot * earlier, axis=1)
    destination = picks * capacity + slots
    source_rows = jnp.arange(row_count * top_count, dtype=jnp.int32) // top_count
    outgoing = jnp.zeros((expert_count * capacity, model_width), jnp.bfloat16)
    outgoing = outgoing.at[destination].set(normed[source_rows])
    sendable = outgoing.reshape(expert_count, 1, capacity, model_width)
    arrived_rows = lax.all_to_all(
        sendable, ("ctx", "heads"), split_axis=0, concat_axis=1, tiled=True
    )
    e_count, n_count, c_count, d_count = arrived_rows.shape
    flat = arrived_rows.reshape(e_count, n_count * c_count, d_count)
    gate_act = jnp.einsum("erd,edf->erf", flat, w_gate, preferred_element_type=jnp.float32)
    up_act = jnp.einsum("erd,edf->erf", flat, w_up, preferred_element_type=jnp.float32)
    hid = (jax.nn.silu(gate_act) * up_act).astype(jnp.bfloat16)
    out_rows = jnp.einsum("erf,efd->erd", hid, w_down, preferred_element_type=jnp.float32)
    finished = out_rows.astype(jnp.bfloat16).reshape(e_count, n_count, c_count, d_count)
    returned = lax.all_to_all(finished, ("ctx", "heads"), split_axis=1, concat_axis=0, tiled=True)
    returned = returned.reshape(expert_count * capacity, model_width)
    picked = returned[destination].reshape(row_count, top_count, model_width).astype(jnp.float32)
    routed = jnp.sum(gate_weights[:, :, None] * picked, axis=1)
    return (hidden_float + routed).astype(jnp.bfloat16)


def ring_pairs(count, step):
    return [(i, (i + step) % count) for i in range(count)]


def partner_pairs(count, bit):
    return [(i, i ^ bit) for i in range(count)]


def after(value, *others):
    return lax.optimization_barrier((value, *others))[0]


def next_place(block, count):
    return lax.ppermute(block, "heads", ring_pairs(count, 1))


def gather_direct(block, count):
    return [block] + [
        lax.ppermute(block, "heads", ring_pairs(count, step)) for step in range(1, count)
    ]


def gather_both_ways(block, count):
    parts = [block] + [None] * (count - 1)
    for step in range(1, count // 2 + 1):
        parts[step] = lax.ppermute(parts[step - 1], "heads", ring_pairs(count, 1))
        if step < count - step:
            before = parts[(1 - step) % count]
            parts[-step] = lax.ppermute(before, "heads", ring_pairs(count, -1))
    return parts


def flip_row(block, ctx_count):
    return lax.ppermute(block, "ctx", partner_pairs(ctx_count, 2))


def flip_core(block, ctx_count):
    return lax.ppermute(block, "ctx", partner_pairs(ctx_count, 1))


def w_out_piece(w_out, group_count):
    piece_rows = w_out.shape[0] // (2 * group_count)
    place = (lax.axis_index("ctx") % 2) * group_count + lax.axis_index("groups")
    return lax.dynamic_slice_in_dim(w_out, place * piece_rows, piece_rows, 0)


def chunk_kernel(head_count, turn, place_ref, *refs):
    near_heads = refs[:head_count]
    far_heads = refs[head_count : 2 * head_count]
    near_tokens, far_tokens, near_out_w, far_out_w, *weights = refs[
        2 * head_count : 2 * head_count + 10
    ]
    outs = refs[2 * head_count + 10 : -10]
    heads_buf, token_buf, mark_buf, w_out_buf, *rest = refs[-10:]
    wide_bufs, narrow_bufs, normed_buf, total_buf, small_sems, weight_sems = rest
    row_count, model_width = outs[0].shape
    slab_rows = row_count * head_count
    experts, mark_rows = narrow_bufs.shape[0], mark_buf.shape[1]
    first = pl.multiple_of(place_ref[turn], row_count)

    pairs = []
    for side, (heads_in, tokens_in) in enumerate(
        ((near_heads, near_tokens), (far_heads, far_tokens))
    ):
        rows = pl.ds(side * row_count, row_count)
        for turns in range(head_count):
            source = heads_in[turns].at[pl.ds(first, row_count)]
            pairs.append((source, heads_buf.at[rows, pl.ds(turns * HDIM, HDIM)]))
        pairs.append((tokens_in, token_buf.at[rows]))
        pairs.append((heads_in[turn].at[pl.ds(slab_rows, mark_rows)], mark_buf.at[side]))
    group_count = near_out_w.shape[0]
    for core, pieces in enumerate((near_out_w, far_out_w)):
        for group in range(group_count):
            slot = place_ref[head_count + 2 + core * group_count + group]
            pairs.append((pieces.at[group], w_out_buf.at[:, slot]))
    small = [
        pltpu.make_async_copy(source, target, small_sems.at[i])
        for i, (source, target) in enumerate(pairs)
    ]
    large = []
    for expert in range(experts):
        targets = (wide_bufs.at[expert, 0], wide_bufs.at[expert, 1], narrow_bufs.at[expert])
        for kind, target in enumerate(targets):
            copy = pltpu.make_async_copy(
                weights[3 * expert + kind].at[0], target, weight_sems.at[3 * expert + kind]
            )
            large.append(copy)

    for copy in small:
        copy.start()
    large[0].start()
    for copy in small:
        copy.wait()
    large[1].start()

    w_out_rows = w_out_buf[...].reshape(head_count * HDIM, model_width)
    attn = jnp.dot(heads_buf[...], w_out_rows, preferred_element_type=jnp.float32)
    hidden = (token_buf[...].astype(jnp.float32) + attn).astype(jnp.bfloat16)
    if len(outs) == 3:
        outs[2][...] = hidden[:row_count]
    normed_buf[...] = normalize(hidden.astype(jnp.float32)).astype(jnp.bfloat16)

    spots = lax.rem(lax.broadcasted_iota(jnp.int32, (mark_rows, HDIM), 0), mark_rows // 2)
    for expert in range(experts):
        chosen = jnp.where(spots == place_ref[head_count + expert], 1.0, 0.0).astype(jnp.bfloat16)
        gating = jnp.concatenate(
            [
                lax.dot_general(
                    mark_buf[side],
                    chosen,
                    (((0,), (0,)), ((), ())),
                    preferred_element_type=jnp.float32,
                )[:, :1]
                for side in range(2)
            ],
            axis=0,
        )
        acts = []
        for kind in range(3):
            step = 3 * expert + kind
            if step + 2 < len(large):
                large[step + 2].start()
            large[step].wait()
            if kind < 2:
                acts.append(
                    jnp.dot(
                        normed_buf[...], wide_bufs[expert, kind], preferred_element_type=jnp.float32
                    )
                )
        hid = (jax.nn.silu(acts[0]) * acts[1]).astype(jnp.bfloat16)
        rows = jnp.dot(hid, narrow_bufs[expert], preferred_element_type=jnp.float32)
        rows = rows.astype(jnp.bfloat16).astype(jnp.float32) * gating
        if expert:
            rows = rows + total_buf[...]
        if expert < experts - 1:
            total_buf[...] = rows
        else:
            rows = rows.astype(jnp.bfloat16)
            outs[0][...] = rows[:row_count]
            outs[1][...] = rows[row_count:]


def run_chunk(turn, place, near_heads, far_heads, near_tokens, far_tokens, w_out, weights):
    row_count, model_width = near_tokens.shape
    head_count = len(near_heads)
    inner = weights[0].shape[2]
    rows = 2 * row_count
    mark_rows = near_heads[0].shape[0] - row_count * head_count
    experts = len(weights) // 3
    outs = 2 if turn else 3
    anywhere = pl.BlockSpec(memory_space=pl.ANY)
    operands = [*near_heads, *far_heads, near_tokens, far_tokens, *w_out, *weights]
    group_count, _, piece_rows, _ = w_out[0].shape
    flops = 2 * rows * model_width * (3 * experts * inner + head_count * HDIM)
    return pl.pallas_call(
        functools.partial(chunk_kernel, head_count, turn),
        out_shape=[jax.ShapeDtypeStruct((row_count, model_width), jnp.bfloat16)] * outs,
        in_specs=[pl.BlockSpec(memory_space=pltpu.SMEM)] + [anywhere] * len(operands),
        out_specs=[pl.BlockSpec(memory_space=pltpu.VMEM)] * outs,
        scratch_shapes=[
            pltpu.VMEM((rows, head_count * HDIM), jnp.bfloat16),
            pltpu.VMEM((rows, model_width), jnp.bfloat16),
            pltpu.VMEM((2, mark_rows, row_count), jnp.bfloat16),
            pltpu.VMEM((head_count, 2 * group_count, piece_rows, model_width), jnp.bfloat16),
            pltpu.VMEM((experts, 2, model_width, inner), jnp.bfloat16),
            pltpu.VMEM((experts, inner, model_width), jnp.bfloat16),
            pltpu.VMEM((rows, model_width), jnp.bfloat16),
            pltpu.VMEM((rows, model_width), jnp.float32),
            pltpu.SemaphoreType.DMA((2 * (head_count + 2 + group_count),)),
            pltpu.SemaphoreType.DMA((3 * experts,)),
        ],
        compiler_params=pltpu.CompilerParams(vmem_limit_bytes=61 * 2**20),
        cost_estimate=pl.CostEstimate(
            flops=flops, bytes_accessed=sum(2 * math.prod(w.shape) for w in weights), transcendentals=0
        ),
        name="chunk",
    )(place, *operands)


def on_device_dense(
    tokens, state_in, past_kv, w_qkv, w_out, w_gate, w_up, w_down, expert_ids, gate_weights
):
    row_count, model_width = tokens.shape
    head_count = lax.axis_size("heads")
    ctx_count = lax.axis_size("ctx")
    group_count = lax.axis_size("groups")
    ctx = lax.axis_index("ctx")
    place = lax.axis_index("heads")
    slab_rows = row_count * head_count
    expert_count = ctx_count * head_count
    starts = [((place - s) % head_count) * row_count for s in range(head_count)]

    hit = expert_ids[:, :, None] == jnp.arange(expert_count, dtype=jnp.int32)[None, None, :]
    dense_weights = jnp.sum(jnp.where(hit, gate_weights[:, :, None], 0.0), axis=1)
    coarse = lax.reduce_precision(dense_weights, 8, 7)
    halves = [coarse, dense_weights - coarse]
    marks = jnp.concatenate(halves, axis=1).astype(jnp.bfloat16).T

    w_flat = w_qkv.reshape(model_width, 3 * HDIM)
    projected = jnp.zeros((slab_rows, 3 * HDIM), jnp.bfloat16)

    def project(projected, s):
        part = jnp.dot(blocks[s], w_flat, preferred_element_type=jnp.float32)
        return lax.dynamic_update_slice_in_dim(projected, part.astype(jnp.bfloat16), starts[s], 0)

    own_expert = ctx * head_count + place
    other_expert = (ctx ^ 1) * head_count + place

    group = lax.axis_index("groups")
    slots = [
        ((ctx % 2) ^ side) * group_count + (group ^ other)
        for side in range(2)
        for other in range(group_count)
    ]
    where = jnp.stack([*starts, own_expert, other_expert, *slots])
    experts = [w_gate, w_up, w_down]
    blocks, across, swapped = [tokens], [], []
    pieces = [w_out_piece(w_out, group_count)] + [None] * (head_count - 1)
    for s in range(head_count - 1):
        blocks.append(next_place(blocks[s], head_count))
        across.append(flip_row(blocks[s], ctx_count))
        swapped.append(flip_core(after(experts[s], blocks[s]), ctx_count))
        projected = project(projected, s)
        for distance in ((1, head_count - 1), range(2, head_count - 1), ())[s]:
            piece = after(pieces[0], blocks[s], swapped[s])
            pieces[distance] = lax.ppermute(piece, "heads", ring_pairs(head_count, distance))
        extra = (pieces, halves)[s - 1] if s else []
        blocks[-1], across[-1], swapped[-1], projected, where, *extra = lax.optimization_barrier(
            (blocks[-1], across[-1], swapped[-1], projected, where, *extra)
        )
        if s == 1:
            halves = [jnp.concatenate(extra, axis=0)]
            if group_count == 2:
                halves.append(lax.ppermute(halves[0], "groups", [(0, 1), (1, 0)]))
    half = jnp.stack(extra, axis=0)
    projected = project(projected, head_count - 1)
    experts = experts + swapped

    query = projected[:, :HDIM]
    keys = projected[:, HDIM : 2 * HDIM]
    values = projected[:, 2 * HDIM :]
    local_state = jnp.dot(keys.T, values, preferred_element_type=jnp.float32)
    arrived = from_behind(projected[:, HDIM:], "ctx", 1)
    start_state = state_in[0]
    packed_state = local_state.astype(jnp.bfloat16)
    for distance in range(2, ctx_count):
        start_state = start_state + from_behind(packed_state, "ctx", distance).astype(jnp.float32)
    start_state = start_state + jnp.dot(
        arrived[:, :HDIM].T, arrived[:, HDIM:], preferred_element_type=jnp.float32
    )
    past = jnp.concatenate([past_kv[0], past_kv[1]], axis=1)
    half = after(half, arrived)
    w_out_halves = [
        part.reshape(group_count, head_count, -1, model_width)
        for part in (half, flip_core(half, ctx_count))
    ]
    previous = jnp.where(ctx == 0, past, arrived)
    all_keys = jnp.concatenate([previous[:, :HDIM], keys], axis=0)
    all_values = jnp.concatenate([previous[:, HDIM:], values], axis=0)
    scale = 1.0 / math.sqrt(HDIM)
    causal = jnp.arange(slab_rows)[:, None] >= jnp.arange(slab_rows)[None, :]
    offsets = jnp.arange(WINDOW + slab_rows)[None, :] - jnp.arange(slab_rows)[:, None]
    in_window = (offsets > 0) & (offsets <= WINDOW)
    carried = jnp.dot(
        query.astype(jnp.float32), start_state, precision=lax.Precision.HIGHEST
    )
    products = jnp.dot(query, all_keys.T, preferred_element_type=jnp.float32)
    inside = jnp.where(causal, products[:, WINDOW:], 0.0).astype(jnp.bfloat16)
    linear = carried + jnp.dot(inside, values, preferred_element_type=jnp.float32)
    scores = jnp.where(in_window, products * scale, -jnp.inf)
    expo = jnp.exp(scores - jnp.max(scores, axis=-1, keepdims=True))
    probs = (expo / jnp.sum(expo, axis=-1, keepdims=True)).astype(jnp.bfloat16)
    window_out = jnp.dot(probs, all_values, preferred_element_type=jnp.float32)
    heads_out = (normalize(linear) + window_out).astype(jnp.bfloat16)

    near_heads = gather_direct(jnp.concatenate([heads_out, marks], axis=0), head_count)
    far_heads = [flip_row(part, ctx_count) for part in near_heads]
    across.append(flip_row(after(blocks[-1], *far_heads), ctx_count))
    across[2] = after(across[2], across[-1])
    carry = None
    for s in list(range(1, head_count)) + [0]:
        near, far, *hidden = run_chunk(
            s, where, near_heads, far_heads, blocks[s], across[s], w_out_halves, experts
        )
        joined = near.astype(jnp.float32) + flip_row(far, ctx_count).astype(jnp.float32)
        if carry is not None:
            joined = joined + carry.astype(jnp.float32)
        if s:
            carry = lax.ppermute(
                joined.astype(jnp.bfloat16), "heads", ring_pairs(head_count, 1)
            )
    return (hidden[0].astype(jnp.float32) + joined).astype(jnp.bfloat16)


def solution(mesh):
    sizes = mesh.shape

    def on_device(*args):
        w_qkv, w_gate, expert_ids = args[3], args[5], args[8]
        expert_count = w_gate.shape[0] * sizes["ctx"] * sizes["heads"]
        slab_rows = args[0].shape[0] * sizes["heads"]
        dense = (
            sizes["ctx"] == 4
            and sizes["heads"] == 4
            and sizes["groups"] <= 2
            and w_gate.shape[0] == 1
            and w_qkv.shape[2] == HDIM
            and slab_rows == WINDOW
            and args[0].shape[0] == HDIM
            and expert_count % 8 == 0
            and expert_count <= 2 * expert_ids.shape[1]
        )
        return (on_device_dense if dense else on_device_routed)(*args)

    return jax.shard_map(
        on_device,
        mesh=mesh,
        in_specs=(
            P(("groups", "ctx", "heads"), None),
            P("heads", "groups", None),
            P(None, "groups", "heads"),
            P(None, None, "heads"),
            P("heads", None),
            P(("ctx", "heads"), None, None),
            P(("ctx", "heads"), None, None),
            P(("ctx", "heads"), None, None),
            P(("groups", "ctx", "heads"), None),
            P(("groups", "ctx", "heads"), None),
        ),
        out_specs=P(("groups", "ctx", "heads"), None),
        check_vma=False,
    )
```
